128 devices in a mesh: lat: 8 (over x, z_hi), lon: 16 (over y, z_lo, core).
Axes of the slice: x: 4, y: 4, z: 4 (z_hi: 2, z_lo: 2; z = z_hi * 2 + z_lo), core: 2. Of those that a mesh axis runs over, the one named last changes fastest.
Arguments:
- ocean_state: bfloat16 [256, 4096, 128], P('lat', 'lon'), may hold values from -6 to 6
- sea_mask: int32 [256, 4096], P('lat', 'lon'), may hold values from 0 to 1, as said below
- depth_kernel: bfloat16 [7, 7, 128], replicated, may hold values from -0.875 to 0.875
- conv_bias: float32 [128], replicated, may hold values from -3 to 3
- norm_gain: float32 [128], replicated, may hold values from 0.5 to 1.5
- w_in: bfloat16 [128, 512], replicated, may hold values from -0.5 to 0.5
- w_out: bfloat16 [512, 128], replicated, may hold values from -0.25 to 0.25
- cotangent: bfloat16 [256, 4096, 128], P('lat', 'lon'), may hold values from -6 to 6
Outputs:
- updated: bfloat16 [256, 4096, 128], P('lat', 'lon')
- grad_state: bfloat16 [256, 4096, 128], P('lat', 'lon')
- grad_kernel: float32 [7, 7, 128], replicated
- grad_bias: float32 [128], replicated
- grad_gain: float32 [128], replicated
- grad_w_in: float32 [128, 512], replicated
- grad_w_out: float32 [512, 128], replicated
The draws below stay inside these ranges and needn't reach their ends.
Inputs may be any that keep to these rules, and one draw needn't show every extreme that they name: `sea_mask`: 1 marks an ocean cell. The tile of one device (32 x 256 cells) holds 6144, 3072 or 768 ocean cells; at each index of lat a quarter of the lon indices have tiles with 6144, a quarter with 3072 and the rest with 768, so each row of tiles holds 43008 ocean cells.
All inputs are finite; a program needn't handle non-finite values.
Results may differ from the reference program's by a relative error of at most 0.014.
Values may be sent and summed in bfloat16 or wider, within the bound.
A program may use at most 128 MiB of HBM per device.

```python
import jax
import jax.numpy as jnp
from jax import lax

C = 128
F = 512
CH = 32
CW = 256
NH = 256
NW = 4096
OCEAN_DEV = 6144
N_LAT = 8
N_LON = 16


def draw_sea_mask(key, part):
    key = jax.random.fold_in(key, 11)
    row_keys = jax.random.split(jax.random.fold_in(key, 1), N_LAT)
    orders = jax.vmap(lambda row_key: jax.random.permutation(row_key, N_LON))(row_keys)
    quarter = N_LON // 4
    counts = jnp.where(orders < quarter, OCEAN_DEV, jnp.where(orders < 2 * quarter, OCEAN_DEV // 2, OCEAN_DEV // 8))
    tile_keys = jax.random.split(jax.random.fold_in(key, 2), N_LAT * N_LON)
    cell_ranks = jax.vmap(lambda tile_key: jax.random.permutation(tile_key, CH * CW))(tile_keys)
    ocean_mask = (cell_ranks < counts.reshape(N_LAT * N_LON, 1)).astype(jnp.int32)
    ocean_mask = ocean_mask.reshape(N_LAT, N_LON, CH, CW).transpose(0, 2, 1, 3)
    return ocean_mask.reshape(CH * N_LAT, CW * N_LON)


def steps_of(own_key, dims, shards, least, largest):
    level = 1.0
    for position, parts in shards:
        heights = jax.random.uniform(jax.random.fold_in(jax.random.fold_in(own_key, 6), position), (parts,), jnp.float32, least / len(shards), largest / len(shards))
        level = level * jnp.repeat(jnp.exp(heights), dims[position] // parts).reshape((-1,) + (1,) * (len(dims) - 1 - position))
    return level


def centred(stream_key, dims, scale, limit, pieces=(), kind=jnp.bfloat16):
    entries = scale * jax.random.normal(stream_key, dims, jnp.float32)
    if pieces:
        entries = entries * steps_of(stream_key, dims, pieces, -0.22, 0.18)
    return jnp.clip(entries, -limit, limit).astype(kind)


def setup_inputs(seed: int = 0) -> dict:
    keys = jax.random.split(jax.random.key(seed), 9)
    ocean_state = centred(keys[0], (NH, NW, C), 1.0, 6.0, ((0, 8), (1, 16)))
    sea_mask = draw_sea_mask(jax.random.fold_in(keys[8], 71), 0)
    depth_kernel = centred(keys[2], (7, 7, C), 49 ** -0.5, 0.875)
    conv_bias = centred(keys[3], (C,), 0.5, 3.0, (), jnp.float32)
    norm_gain = jnp.clip(jax.random.uniform(keys[4], (C,), jnp.float32, 0.5, 1.5), 0.5, 1.5)
    w_in = centred(keys[5], (C, F), C ** -0.5, 0.5)
    w_out = centred(keys[6], (F, C), F ** -0.5, 0.25)
    cotangent = centred(keys[7], (NH, NW, C), 1.0, 6.0, ((0, 8), (1, 16)))
    return dict(ocean_state=ocean_state, sea_mask=sea_mask, depth_kernel=depth_kernel, conv_bias=conv_bias, norm_gain=norm_gain, w_in=w_in, w_out=w_out, cotangent=cotangent)


epsilon = 1e-06
root_half = 0.7978845608028654
cubic_coef = 0.044715
group_width = 8
block_cells = 8192

def gelu_pair(preact):
    inner_arg = root_half * (preact + cubic_coef * preact * preact * preact)
    tanh_val = jnp.tanh(inner_arg)
    active = 0.5 * preact * (1.0 + tanh_val)
    derivative = 0.5 * (1.0 + tanh_val) + 0.5 * preact * (1.0 - tanh_val * tanh_val) * root_half * (1.0 + 3.0 * cubic_coef * preact * preact)
    return (active, derivative)

def normalize(conv_rows, norm_gain):
    centre = lax.optimization_barrier(jnp.mean(conv_rows, axis=-1, keepdims=True))
    shifted = conv_rows - centre
    variance = lax.optimization_barrier(jnp.mean(shifted * shifted, axis=-1, keepdims=True))
    inv_std = 1.0 / jnp.sqrt(variance + epsilon)
    unit_norm = shifted * inv_std
    return (unit_norm, inv_std, (unit_norm * norm_gain).astype(jnp.bfloat16))

def column_mlp(normed, upstream, w_in, w_out):
    preact = jnp.dot(normed, w_in, preferred_element_type=jnp.float32)
    active, derivative = gelu_pair(preact)
    hidden = active.astype(jnp.bfloat16)
    mixed_out = jnp.dot(hidden, w_out, preferred_element_type=jnp.float32).astype(jnp.bfloat16)
    back_hidden = lax.dot_general(upstream, w_out, (((1,), (1,)), ((), ())), preferred_element_type=jnp.float32)
    back_pre = (back_hidden * derivative).astype(jnp.bfloat16)
    back_normed = lax.dot_general(back_pre, w_in, (((1,), (1,)), ((), ())), preferred_element_type=jnp.float32).astype(jnp.bfloat16)
    in_part = lax.dot_general(normed, back_pre, (((0,), (0,)), ((), ())), preferred_element_type=jnp.float32)
    out_part = lax.dot_general(hidden, upstream, (((0,), (0,)), ((), ())), preferred_element_type=jnp.float32)
    return (mixed_out, back_normed, in_part, out_part)

def norm_back(back_normed, unit_norm, inv_std, norm_gain):
    back_float = back_normed.astype(jnp.float32)
    scaled = back_float * norm_gain
    mean_one = lax.optimization_barrier(jnp.mean(scaled, axis=-1, keepdims=True))
    mean_two = lax.optimization_barrier(jnp.mean(scaled * unit_norm, axis=-1, keepdims=True))
    back_conv = ((scaled - mean_one - unit_norm * mean_two) * inv_std).astype(jnp.bfloat16)
    gain_part = lax.optimization_barrier(jnp.sum(back_float * unit_norm, axis=0))
    return (back_conv, gain_part)

def extend(field_part):
    upper_rows = field_part[-3:][::-1, ::-1]
    lower_rows = jnp.zeros((3,) + field_part.shape[1:], field_part.dtype)
    stacked = jnp.concatenate([lower_rows, field_part, upper_rows], axis=0)
    return jnp.concatenate([stacked[:, -3:], stacked, stacked[:, :3]], axis=1)

def depthwise(extended, tap_block, out_rows, out_cols):
    running = jnp.zeros((out_rows, out_cols, extended.shape[2]), jnp.float32)
    for row_tap in range(7):
        for col_tap in range(7):
            window = extended[row_tap:row_tap + out_rows, col_tap:col_tap + out_cols].astype(jnp.float32)
            running = running + window * tap_block[row_tap, col_tap].astype(jnp.float32)
    return running

def reference(ocean_state, sea_mask, depth_kernel, conv_bias, norm_gain, w_in, w_out, cotangent):
    grid_rows, grid_cols, channels = ocean_state.shape
    group_count = channels // group_width
    group_ids = jnp.arange(group_count, dtype=jnp.int32)
    grad_scale = 1.0 / jnp.sqrt(jnp.float32(NH * NW))

    def conv_group(group_index):
        first_chan = group_index * group_width
        field_part = lax.dynamic_slice_in_dim(ocean_state, first_chan, group_width, 2)
        tap_block = lax.dynamic_slice_in_dim(depth_kernel, first_chan, group_width, 2)
        bias_part = lax.dynamic_slice_in_dim(conv_bias, first_chan, group_width, 0)
        return depthwise(extend(field_part), tap_block, grid_rows, grid_cols) + bias_part
    conv_out = lax.map(conv_group, group_ids)
    conv_out = jnp.moveaxis(conv_out, 0, 2).reshape(grid_rows, grid_cols, channels)
    block_count = grid_rows * grid_cols // block_cells
    flat_conv = conv_out.reshape(block_count, block_cells, channels)
    flat_sea = sea_mask.reshape(block_count, block_cells, 1)
    flat_cot = cotangent.reshape(block_count, block_cells, channels)

    def cell_block(inputs):
        conv_rows, sea_rows, cot_rows = inputs
        unit_norm, inv_std, normed = normalize(conv_rows, norm_gain)
        upstream = jnp.where(sea_rows == 1, cot_rows, jnp.zeros_like(cot_rows))
        mixed_out, back_normed, in_part, out_part = column_mlp(normed, upstream, w_in, w_out)
        back_conv, gain_part = norm_back(back_normed, unit_norm, inv_std, norm_gain)
        return (mixed_out, back_conv, gain_part, in_part, out_part)
    mixed_out, back_conv, gain_parts, in_parts, out_parts = lax.map(cell_block, (flat_conv, flat_sea, flat_cot))
    mixed_out = mixed_out.reshape(grid_rows, grid_cols, channels)
    back_conv = back_conv.reshape(grid_rows, grid_cols, channels)
    sea_cube = sea_mask[:, :, None] == 1
    updated = (ocean_state.astype(jnp.float32) + jnp.where(sea_cube, mixed_out.astype(jnp.float32), 0.0)).astype(jnp.bfloat16)

    def back_group(group_index):
        first_chan = group_index * group_width
        field_part = lax.dynamic_slice_in_dim(ocean_state, first_chan, group_width, 2)
        tap_block = lax.dynamic_slice_in_dim(depth_kernel, first_chan, group_width, 2)
        back_part = lax.dynamic_slice_in_dim(back_conv, first_chan, group_width, 2).astype(jnp.float32)
        extended = extend(field_part)
        kernel_rows = []
        for row_tap in range(7):
            kernel_cols = []
            for col_tap in range(7):
                window = extended[row_tap:row_tap + grid_rows, col_tap:col_tap + grid_cols].astype(jnp.float32)
                kernel_cols.append(lax.optimization_barrier(jnp.sum(window * back_part, axis=(0, 1))))
            kernel_rows.append(jnp.stack(kernel_cols))
        primal, pullback = jax.vjp(lambda moved_field: depthwise(extend(moved_field), tap_block, grid_rows, grid_cols), field_part.astype(jnp.float32))
        return (pullback(back_part)[0], jnp.stack(kernel_rows))
    field_grads, kernel_grads = lax.map(back_group, group_ids)
    field_grads = jnp.moveaxis(field_grads, 0, 2).reshape(grid_rows, grid_cols, channels)
    kernel_grads = jnp.moveaxis(kernel_grads, 0, 2).reshape(7, 7, channels)
    grad_state = (cotangent.astype(jnp.float32) + field_grads).astype(jnp.bfloat16)
    grad_bias = lax.optimization_barrier(jnp.sum(back_conv.astype(jnp.float32), axis=(0, 1))) * grad_scale
    grad_gain = lax.optimization_barrier(jnp.sum(gain_parts, axis=0)) * grad_scale
    grad_w_in = lax.optimization_barrier(jnp.sum(in_parts, axis=0)) * grad_scale
    grad_w_out = lax.optimization_barrier(jnp.sum(out_parts, axis=0)) * grad_scale
    grad_kernel = kernel_grads * grad_scale
    return (updated, grad_state, grad_kernel, grad_bias, grad_gain, grad_w_in, grad_w_out)
```

```python
import functools
import jax
import jax.numpy as jnp
from jax import lax
from jax.experimental import pallas as pl
from jax.experimental.pallas import tpu as pltpu
from jax.sharding import PartitionSpec as P

MESH = pl.DeviceIdType.MESH
bf16 = jnp.bfloat16
f32 = jnp.float32
epsilon = 1e-06
root_half = 0.7978845608028654
cubic_coef = 0.044715

C = 128
ROWS = 32
COLS = 256
HID = 512
EXT = 22 * 16
VLIM = 60 * 1024 * 1024


def iota2(shape, dim):
    return lax.broadcasted_iota(jnp.int32, shape, dim)


def one_hot(hit):
    return jnp.where(hit, 1.0, 0.0).astype(bf16)


def place(rows, edges):
    o = iota2((rows, 1), 0)
    if edges:
        o = jnp.where(o >= 48, o + 256, o)
    return (o % 16) * 16 + o // 16 - 3


def swap(o):
    return (o % 16) * 16 + o // 16


def dot(a, b):
    return jnp.dot(a, b, preferred_element_type=f32)


def dot_t(a, b):
    return lax.dot_general(a, b, (((0,), (0,)), ((), ())), preferred_element_type=f32)


def conv_taps(ext, row, taps, k0, nk):
    acc = [None] * nk
    for a in range(7):
        win = [ext[row + a, k0 + kk] for kk in range(nk + 6)]
        w = [taps[a * 7 + b] for b in range(7)]
        for k in range(nk):
            p = win[k] * w[0]
            for b in range(1, 7):
                p = p + win[k + b] * w[b]
            p = p.astype(f32)
            acc[k] = p if acc[k] is None else acc[k] + p
    return acc


def gelu_parts(v):
    u = v * v
    t = jnp.tanh(v * (root_half + (root_half * cubic_coef) * u))
    h = 0.5 * t + 0.5
    act = v * h
    der = h + act * (1.0 - h) * (2.0 * root_half + (6.0 * root_half * cubic_coef) * u)
    return act, der


R = 2
M = R * COLS
NB = ROWS // R


def main_kernel(flags, x, hr, hc, mask, cot, taps1, bias, gain, w_in, w_in_t, w_out, w_out_t,
                upd, back, edge, xp, gin, gout, small,
                ext, taps, perm, norm_s, unit_s, inv_s, up_s, mask_s, xs_s):
    i = pl.program_id(0)

    @pl.when(i == 0)
    def _():
        for t in range(49):
            taps[t] = jnp.broadcast_to(taps1[t:t + 1], (16, C))
        col = iota2((1, COLS), 1)
        amat = one_hot(place(EXT, False) == col)
        h = iota2((1, 32), 1)
        bmat = one_hot(place(96, True) == jnp.where(h < 16, h - 16, 240 + h))
        perm[...] = one_hot(swap(iota2((COLS, 1), 0)) == col)

        def build(am, bm, main, side):
            full = dot(am, main)
            rim = dot(bm, side)
            return jnp.concatenate([full[:48] + rim[:48], full[48:304], full[304:] + rim[48:]], axis=0).astype(bf16)

        def inner(j, _):
            main = jnp.concatenate([x[2 * j], x[2 * j + 1]], axis=-1)
            side = jnp.concatenate([hc[2 * j + 3], hc[2 * j + 4]], axis=-1)
            full = build(amat, bmat, main, side)
            ext[2 * j + 3] = full[:, :C].reshape(22, 16, C)
            ext[2 * j + 4] = full[:, C:].reshape(22, 16, C)
            return 0

        lax.fori_loop(0, ROWS // 2, inner, 0)
        is_bottom = flags[0] == 1
        is_top = flags[1] == 1
        for e in range(3):
            main = jnp.where(is_bottom, jnp.zeros((COLS, C), bf16), hr[e])
            side = jnp.where(is_bottom, jnp.zeros((32, C), bf16), hc[e])
            ext[e] = build(amat, bmat, main, side).reshape(22, 16, C)
        acol = jnp.where(is_top, 255 - col, col)
        amat_t = one_hot(place(EXT, False) == acol)
        hpos = jnp.where(is_top, jnp.where(h < 16, -1 - h, 287 - h), jnp.where(h < 16, h - 16, 240 + h))
        bmat_t = one_hot(place(96, True) == hpos)
        for m in range(3):
            src = jnp.where(is_top, 2 - m, m)
            ext[35 + m] = build(amat_t, bmat_t, hr[3 + src], hc[35 + src]).reshape(22, 16, C)
        norm_s[...] = jnp.zeros_like(norm_s)
        unit_s[...] = jnp.zeros_like(unit_s)
        inv_s[...] = jnp.zeros_like(inv_s)
        up_s[...] = jnp.zeros_like(up_s)
        mask_s[...] = jnp.zeros_like(mask_s)
        xs_s[...] = jnp.zeros_like(xs_s)
        gin[...] = jnp.zeros_like(gin)
        gout[...] = jnp.zeros_like(gout)
        small[...] = jnp.zeros_like(small)

    other = 1 - i % 2
    slot = i % 2
    normed = norm_s[other]
    upstream = up_s[other]
    mixed = None
    bn = None
    for f in range(0, HID, 256):
        pre = dot(normed, w_in[:, f:f + 256])
        bh = dot(upstream, w_out_t[:, f:f + 256])
        act, der = gelu_parts(pre)
        hid = act.astype(bf16)
        bp = (bh * der).astype(bf16)
        mx = dot(hid, w_out[f:f + 256])
        bx = dot(bp, w_in_t[f:f + 256])
        mixed = mx if mixed is None else mixed + mx
        bn = bx if bn is None else bn + bx
        gin[:, f:f + 256] += dot_t(normed, bp)
        gout[:, f:f + 256] += dot_t(upstream, hid)
    mixed = (mixed * mask_s[other]).astype(bf16)
    pm = perm[...]
    unit = unit_s[other]
    bnf = bn.astype(bf16).astype(f32)
    g = bnf * gain[...]
    m1 = jnp.mean(g, axis=-1, keepdims=True)
    m2 = jnp.mean(g * unit, axis=-1, keepdims=True)
    bc = ((g - m1 - unit * m2) * inv_s[other]).astype(bf16)
    small[0:8] += jnp.sum((bnf * unit).reshape(M // 8, 8, C), axis=0)
    small[8:16] += jnp.sum(bc.astype(f32).reshape(M // 8, 8, C), axis=0)
    h32 = iota2((32, 1), 0)
    sel = one_hot(jnp.where(h32 < 16, h32, 224 + h32) == swap(iota2((1, COLS), 1)))
    for r in range(R):
        sl = slice(r * COLS, (r + 1) * COLS)
        nat = dot(pm, mixed[sl])
        upd[r] = (xs_s[other, sl].astype(f32) + nat).astype(bf16)
        back[r] = bc[sl]
        edge[r] = dot(sel, bc[sl]).astype(bf16)

    nb = jnp.minimum(i, NB - 1)
    ones = jnp.ones((COLS, C), bf16)
    for r in range(R):
        row = nb * R + r
        sl = slice(r * COLS, (r + 1) * COLS)
        accs = []
        for k0 in (0, 8):
            accs += conv_taps(ext, row, taps, k0, 8)
        conv = jnp.concatenate([a + bias[...] for a in accs], axis=0)
        centre = jnp.mean(conv, axis=-1, keepdims=True)
        shifted = conv - centre
        var = jnp.mean(shifted * shifted, axis=-1, keepdims=True)
        inv = lax.rsqrt(var + epsilon)
        unit = shifted * inv
        unit_s[slot, sl] = unit
        inv_s[slot, sl] = jnp.broadcast_to(inv, (COLS, C))
        norm_s[slot, sl] = (unit * gain[...]).astype(bf16)
        pmask = pm * mask[pl.ds(row, 1), :].astype(f32).astype(bf16)
        both = dot(pmask, jnp.concatenate([cot[r], ones], axis=-1))
        up_s[slot, sl] = both[:, :C].astype(bf16)
        mask_s[slot, sl] = both[:, C:]
        xs_s[slot, sl] = x[row]
        xp[r] = ext[row + 3, 3:19].reshape(COLS, C)


def main_call(flags, x, hr, hc, mask, cot, depth_kernel, bias, gain, w_in, w_out):
    vm = pl.BlockSpec(memory_space=pltpu.VMEM)
    now = lambda i: (jnp.minimum(i, NB - 1), 0, 0)
    past = lambda i: (jnp.maximum(i - 1, 0), 0, 0)
    whole2 = lambda i: (0, 0)
    tile = jax.ShapeDtypeStruct((ROWS, COLS, C), bf16)
    return pl.pallas_call(
        main_kernel,
        grid=(NB + 1,),
        in_specs=[pl.BlockSpec(memory_space=pltpu.SMEM), vm, vm, vm, vm,
                  pl.BlockSpec((R, COLS, C), now), vm, vm, vm, vm, vm, vm, vm],
        out_specs=[pl.BlockSpec((R, COLS, C), past), pl.BlockSpec((R, COLS, C), past),
                   pl.BlockSpec((R, 32, C), past), pl.BlockSpec((R, COLS, C), now),
                   pl.BlockSpec((C, HID), whole2), pl.BlockSpec((C, HID), whole2), pl.BlockSpec((16, C), whole2)],
        out_shape=[tile, tile, jax.ShapeDtypeStruct((ROWS, 32, C), bf16), tile,
                   jax.ShapeDtypeStruct((C, HID), f32), jax.ShapeDtypeStruct((C, HID), f32),
                   jax.ShapeDtypeStruct((16, C), f32)],
        scratch_shapes=[
            pltpu.VMEM((38, 22, 16, C), bf16), pltpu.VMEM((49, 16, C), bf16), pltpu.VMEM((COLS, COLS), bf16),
            pltpu.VMEM((2, M, C), bf16), pltpu.VMEM((2, M, C), f32), pltpu.VMEM((2, M, C), f32),
            pltpu.VMEM((2, M, C), bf16), pltpu.VMEM((2, M, C), f32), pltpu.VMEM((2, M, C), bf16)],
        compiler_params=pltpu.CompilerParams(vmem_limit_bytes=VLIM),
        name="conv_norm_mlp",
    )(flags, x, hr, hc, mask, cot, depth_kernel.reshape(49, C), bias.reshape(1, C), gain.reshape(1, C),
      w_in, w_in.T, w_out, w_out.T)


def back_kernel(flags, back, hr, hc, xp, cot, taps1, out, gk, ext, fold, taps, perm, gks):
    i = pl.program_id(0)

    @pl.when(i == 0)
    def _():
        for t in range(49):
            taps[t] = jnp.broadcast_to(taps1[t:t + 1], (16, C))
        for t in range(49):
            taps[49 + t] = taps[48 - t]
        col = swap(iota2((1, COLS), 1))
        place_e = place(96, True)
        amat = one_hot(place_e == col)
        h = iota2((1, 32), 1)
        bmat = one_hot(place_e == jnp.where(h < 16, h - 16, 240 + h))
        perm[...] = one_hot(swap(iota2((COLS, 1), 0)) == iota2((1, COLS), 1))
        gks[...] = jnp.zeros_like(gks)

        def put(dst, e, main, rim):
            rim = rim.astype(bf16).reshape(6, 16, C)
            dst[e, 3:19] = main.reshape(16, 16, C)
            dst[e, 0:3] = rim[0:3]
            dst[e, 19:22] = rim[3:6]

        def inner(j, _):
            b0 = back[2 * j]
            b1 = back[2 * j + 1]
            main = jnp.concatenate([b0, b1], axis=-1)
            side = jnp.concatenate([hc[2 * j + 3], hc[2 * j + 4]], axis=-1)
            rim = dot(amat, main) + dot(bmat, side)
            put(ext, 2 * j + 3, b0, rim[:, :C])
            put(ext, 2 * j + 4, b1, rim[:, C:])
            return 0

        lax.fori_loop(0, ROWS // 2, inner, 0)
        is_bottom = flags[0] == 1
        is_top = flags[1] == 1
        zero_m = jnp.zeros((COLS, C), bf16)
        zero_s = jnp.zeros((32, C), bf16)
        for e in range(3):
            main = jnp.where(is_bottom, zero_m, hr[e])
            put(ext, e, main, dot(amat, main) + dot(bmat, jnp.where(is_bottom, zero_s, hc[e])))
            main = jnp.where(is_top, zero_m, hr[3 + e])
            put(ext, 35 + e, main, dot(amat, main) + dot(bmat, jnp.where(is_top, zero_s, hc[35 + e])))
        amat_f = one_hot(place(EXT, False) == 255 - col)
        bmat_f = one_hot(place_e == jnp.where(h < 16, -1 - h, 287 - h))
        for m in range(3):
            full = dot(amat_f, hr[5 - m])
            rim = dot(bmat_f, hc[37 - m])
            full = jnp.concatenate([full[:48] + rim[:48], full[48:304], full[304:] + rim[48:]], axis=0).astype(bf16)
            fold[m] = jnp.where(is_top, full, jnp.zeros_like(full)).reshape(22, 16, C)

    def add_row(src, pairs, r, k0, nk, acc, tap0):
        xv = [xp[r, (k0 + k) * 16:(k0 + k + 1) * 16] for k in range(nk)]
        for row, a in pairs:
            win = [src[row, k0 + kk] for kk in range(nk + 6)]
            w = [taps[tap0 + a * 7 + b] for b in range(7)]
            for k in range(nk):
                p = win[k] * w[0]
                for b in range(1, 7):
                    p = p + win[k + b] * w[b]
                p = p.astype(f32)
                acc[k] = p if acc[k] is None else acc[k] + p
            for b in range(7):
                q = win[b] * xv[0]
                for k in range(1, nk):
                    q = q + win[k + b] * xv[k]
                t = a * 7 + b
                q = q.astype(f32)
                gks[(48 - t) if tap0 else t] += q[:8] + q[8:]

    for r in range(RB):
        row = i * RB + r
        accs = []
        for k0 in (0, 8):
            acc = [None] * 8
            add_row(ext, [(row + a, a) for a in range(7)], r, k0, 8, acc, 49)
            accs += acc
        conv = jnp.concatenate(accs, axis=0)
        out[r] = (cot[r].astype(f32) + dot(perm[...], conv.astype(bf16))).astype(bf16)

    @pl.when((i == ROWS // RB - 1) & (flags[1] == 1))
    def _():
        for t in range(3):
            r = RB - 3 + t
            accs = []
            for k0 in (0, 8):
                acc = [None] * 8
                add_row(fold, [(m, 6 - t + m) for m in range(t + 1)], r, k0, 8, acc, 0)
                accs += acc
            conv = jnp.concatenate(accs, axis=0)
            out[r] = (out[r].astype(f32) + dot(perm[...], conv.astype(bf16))).astype(bf16)

    @pl.when(i == ROWS // RB - 1)
    def _():
        gk[...] = jnp.zeros_like(gk)
        for t in range(49):
            gk[t:t + 1] = jnp.sum(gks[t], axis=0, keepdims=True)


RB = 4


def back_call(flags, back, hr, hc, xp, cot, depth_kernel):
    vm = pl.BlockSpec(memory_space=pltpu.VMEM)
    blk = pl.BlockSpec((RB, COLS, C), lambda i: (i, 0, 0))
    return pl.pallas_call(
        back_kernel,
        grid=(ROWS // RB,),
        in_specs=[pl.BlockSpec(memory_space=pltpu.SMEM), vm, vm, vm, blk, blk, vm],
        out_specs=[blk, pl.BlockSpec((64, C), lambda i: (0, 0))],
        out_shape=[jax.ShapeDtypeStruct((ROWS, COLS, C), bf16), jax.ShapeDtypeStruct((64, C), f32)],
        scratch_shapes=[
            pltpu.VMEM((38, 22, 16, C), bf16), pltpu.VMEM((3, 22, 16, C), bf16), pltpu.VMEM((98, 16, C), bf16),
            pltpu.VMEM((COLS, COLS), bf16), pltpu.VMEM((49, 8, C), f32)],
        compiler_params=pltpu.CompilerParams(vmem_limit_bytes=VLIM),
        name="conv_back",
    )(flags, back, hr, hc, xp, cot, depth_kernel.reshape(49, C))


def neighbours(lat, lon):
    nl = lax.axis_size("lon")
    top = lat == lax.axis_size("lat") - 1
    low = lat > 0
    left = lax.rem(lon + nl - 1, nl)
    right = lax.rem(lon + 1, nl)
    up = jnp.where(top, lat, lat + 1)
    down = jnp.where(low, lat - 1, lat)
    f0 = jnp.where(top, nl - 1 - lon, lon)
    fl = jnp.where(top, lax.rem(nl - lon, nl), left)
    fr = jnp.where(top, lax.rem(2 * nl - 2 - lon, nl), right)
    return top, low, up, down, left, right, f0, fl, fr


def halo_kernel(rows, lcols, rcols, hr, hc, send, recv):
    lat = lax.axis_index("lat")
    lon = lax.axis_index("lon")
    top, low, up, down, left, right, f0, fl, fr = neighbours(lat, lon)
    far_l = jnp.logical_not(top & (fl == lon))
    far_r = jnp.logical_not(top & (fr == lon))
    inner = jnp.logical_not(top)

    def greet(a, b):
        pl.semaphore_signal(barrier, inc=1, device_id=(a, b), device_id_type=MESH)

    barrier = pltpu.get_barrier_semaphore()
    greet(lat, left)
    greet(lat, right)
    greet(up, f0)

    @pl.when(far_l)
    def _():
        greet(up, fl)

    @pl.when(far_r)
    def _():
        greet(up, fr)

    @pl.when(low)
    def _():
        greet(down, lon)
        greet(down, left)
        greet(down, right)

    count = 3 + jnp.where(far_l, 1, 0) + jnp.where(far_r, 1, 0) + jnp.where(low, 3, 0)
    pl.semaphore_wait(barrier, count)

    def copy(src, dst, s, slot, a, b):
        return pltpu.make_async_remote_copy(src_ref=src, dst_ref=dst, send_sem=send.at[s], recv_sem=recv.at[slot],
                                            device_id=(a, b), device_id_type=MESH)

    last = pl.ds(ROWS - 3, 3)
    first = pl.ds(0, 3)
    lo, mid, hi = pl.ds(0, 3), pl.ds(3, ROWS), pl.ds(ROWS + 3, 3)
    to_l, to_r = pl.ds(0, 16), pl.ds(16, 16)
    c_right = copy(rcols, hc.at[mid, to_l], 2, 2, lat, right)
    c_left = copy(lcols, hc.at[mid, to_r], 3, 3, lat, left)
    up_n = copy(rows.at[last], hr.at[pl.ds(0, 3)], 1, 0, up, f0)
    up_f = copy(rows.at[last], hr.at[pl.ds(3, 3)], 1, 1, up, f0)
    ul_n = copy(lcols.at[last], hc.at[lo, to_r], 6, 5, up, fl)
    ul_f = copy(lcols.at[last], hc.at[hi, to_l], 6, 6, up, fl)
    ur_n = copy(rcols.at[last], hc.at[lo, to_l], 7, 4, up, fr)
    ur_f = copy(rcols.at[last], hc.at[hi, to_r], 7, 7, up, fr)
    dn = copy(rows.at[first], hr.at[pl.ds(3, 3)], 0, 1, down, lon)
    dl = copy(lcols.at[first], hc.at[hi, to_r], 4, 7, down, left)
    dr = copy(rcols.at[first], hc.at[hi, to_l], 5, 6, down, right)
    own_l = pltpu.make_async_copy(lcols.at[last], hc.at[hi, to_l], send.at[6])
    own_r = pltpu.make_async_copy(rcols.at[last], hc.at[hi, to_r], send.at[7])

    @pl.when(inner)
    def _():
        up_n.start()
        ul_n.start()
        ur_n.start()

    @pl.when(top)
    def _():
        up_f.start()

    @pl.when(top & far_l)
    def _():
        ul_f.start()

    @pl.when(top & far_r)
    def _():
        ur_f.start()

    @pl.when(jnp.logical_not(far_l))
    def _():
        own_l.start()

    @pl.when(jnp.logical_not(far_r))
    def _():
        own_r.start()

    @pl.when(low)
    def _():
        dn.start()
        dl.start()
        dr.start()

    c_right.start()
    c_left.start()
    c_right.wait()
    c_left.wait()

    dn.wait_recv()

    @pl.when(far_l)
    def _():
        dr.wait_recv()

    @pl.when(far_r)
    def _():
        dl.wait_recv()

    @pl.when(jnp.logical_not(far_l))
    def _():
        own_l.wait()

    @pl.when(jnp.logical_not(far_r))
    def _():
        own_r.wait()

    @pl.when(low)
    def _():
        up_n.wait_recv()
        ul_n.wait_recv()
        ur_n.wait_recv()
        dn.wait_send()
        dl.wait_send()
        dr.wait_send()

    up_n.wait_send()

    @pl.when(far_l)
    def _():
        ul_n.wait_send()

    @pl.when(far_r)
    def _():
        ur_n.wait_send()


def halo_call(rows, lcols, rcols, ident):
    hbm = pl.BlockSpec(memory_space=pl.ANY)
    return pl.pallas_call(
        halo_kernel,
        in_specs=[hbm] * 3,
        out_specs=[hbm] * 2,
        out_shape=[jax.ShapeDtypeStruct((6, COLS, C), bf16), jax.ShapeDtypeStruct((ROWS + 6, 32, C), bf16)],
        scratch_shapes=[pltpu.SemaphoreType.DMA((8,)), pltpu.SemaphoreType.DMA((8,))],
        compiler_params=pltpu.CompilerParams(collective_id=ident, has_side_effects=True),
        name="halo",
    )(rows, lcols, rcols)


N_LON = 16
N_LAT = 8
SEG = 64


def sum_kernel(w, small, scale, out_w, out_s, wb, sb, r1, r2, r3, c2, s1, q1, s2, q2, s3, q3):
    lat = lax.axis_index("lat")
    lon = lax.axis_index("lon")
    barrier = pltpu.get_barrier_semaphore()

    def greet_lon(d, _):
        pl.semaphore_signal(barrier, inc=1, device_id=(lat, lax.rem(lon + d, N_LON)), device_id_type=MESH)
        return 0

    def greet_lat(d, _):
        pl.semaphore_signal(barrier, inc=1, device_id=(lax.rem(lat + d, N_LAT), lon), device_id_type=MESH)
        return 0

    lax.fori_loop(1, N_LON, greet_lon, 0)
    lax.fori_loop(1, N_LAT, greet_lat, 0)
    for c in range(N_LON):
        wb[c, 0:SEG] = w[c * SEG:(c + 1) * SEG].astype(bf16)
        wb[c, SEG:2 * SEG] = small[...].astype(bf16)
    pl.semaphore_wait(barrier, N_LON + N_LAT - 2)

    def first(d):
        to = lax.rem(lon + d, N_LON)
        return pltpu.make_async_remote_copy(src_ref=wb.at[to], dst_ref=r1.at[d], send_sem=s1.at[d], recv_sem=q1.at[d],
                                            device_id=(lat, to), device_id_type=MESH)

    def second(d):
        return pltpu.make_async_remote_copy(src_ref=c2, dst_ref=r2.at[lat], send_sem=s2.at[d], recv_sem=q2.at[d],
                                            device_id=(lax.rem(lat + d, N_LAT), lon), device_id_type=MESH)

    def third(d):
        return pltpu.make_async_remote_copy(src_ref=sb, dst_ref=r3.at[lon], send_sem=s3.at[d], recv_sem=q3.at[d],
                                            device_id=(lat, lax.rem(lon + d, N_LON)), device_id_type=MESH)

    def run(make, n):
        def go(d, _):
            make(d).start()
            return 0

        lax.fori_loop(1, n, go, 0)

    def arrive(make, n):
        def go(d, _):
            make(d).wait()
            return 0

        lax.fori_loop(1, n, go, 0)

    run(first, N_LON)
    arrive(first, N_LON)
    total = wb[lon].astype(f32)
    for d in range(1, N_LON):
        total = total + r1[d].astype(f32)
    c2[...] = total.astype(bf16)
    run(second, N_LAT)
    r2[lat] = c2[...]
    arrive(second, N_LAT)
    total = r2[0].astype(f32)
    for d in range(1, N_LAT):
        total = total + r2[d].astype(f32)
    total = total * scale[0]
    sb[...] = total[:SEG].astype(bf16)
    run(third, N_LON)
    out_s[...] = total[SEG:]
    r3[lon] = sb[...]
    arrive(third, N_LON)
    for c in range(N_LON):
        out_w[c * SEG:(c + 1) * SEG] = r3[c].astype(f32)


def sum_call(w, small, scale):
    vm = pl.BlockSpec(memory_space=pltpu.VMEM)
    dma = pltpu.SemaphoreType.DMA
    return pl.pallas_call(
        sum_kernel,
        in_specs=[vm, vm, pl.BlockSpec(memory_space=pltpu.SMEM)],
        out_specs=[vm, vm],
        out_shape=[jax.ShapeDtypeStruct((1024, C), f32), jax.ShapeDtypeStruct((SEG, C), f32)],
        scratch_shapes=[
            pltpu.VMEM((N_LON, 2 * SEG, C), bf16), pltpu.VMEM((SEG, C), bf16),
            pltpu.VMEM((N_LON, 2 * SEG, C), bf16), pltpu.VMEM((N_LAT, 2 * SEG, C), bf16), pltpu.VMEM((N_LON, SEG, C), bf16),
            pltpu.VMEM((2 * SEG, C), bf16),
            dma((N_LON,)), dma((N_LON,)), dma((N_LAT,)), dma((N_LAT,)), dma((N_LON,)), dma((N_LON,))],
        compiler_params=pltpu.CompilerParams(collective_id=2, has_side_effects=True, vmem_limit_bytes=VLIM),
        name="sum_grads",
    )(w, small, scale)


def body(ocean_state, sea_mask, depth_kernel, conv_bias, norm_gain, w_in, w_out, cotangent):
    lat = lax.axis_index("lat")
    flags = jnp.stack([lat == 0, lat == lax.axis_size("lat") - 1]).astype(jnp.int32)
    hr, hc = halo_call(ocean_state, ocean_state[:, :16], ocean_state[:, COLS - 16:], 0)
    upd, back, edge, xp, gin, gout, small = main_call(
        flags, ocean_state, hr, hc, sea_mask, cotangent, depth_kernel, conv_bias, norm_gain, w_in, w_out)
    hr2, hc2 = halo_call(back, edge[:, :16], edge[:, 16:], 1)
    grad_state, gk = back_call(flags, back, hr2, hc2, xp, cotangent, depth_kernel)
    cells = COLS * ROWS * lax.axis_size("lat") * lax.axis_size("lon")
    scale = 1.0 / jnp.sqrt(jnp.full((1,), cells, f32))
    extra = jnp.concatenate([gk[:49], jnp.sum(small[:8], axis=0, keepdims=True),
                             jnp.sum(small[8:], axis=0, keepdims=True), jnp.zeros((13, C), f32)], axis=0)
    w = jnp.concatenate([gin.reshape(512, C), gout.reshape(512, C)], axis=0)
    out_w, out_s = sum_call(w, extra, scale)
    return (upd, grad_state, out_s[:49].reshape(7, 7, C), out_s[50], out_s[49],
            out_w[:512].reshape(C, HID), out_w[512:].reshape(C, HID).T)


def solution(mesh):
    tile = P("lat", "lon", None)
    return jax.shard_map(
        body,
        mesh=mesh,
        in_specs=(tile, P("lat", "lon"), P(), P(), P(), P(), P(), tile),
        out_specs=(tile, tile, P(), P(), P(), P(), P()),
        check_vma=False,
    )
```

```python
import functools
import jax
import jax.numpy as jnp
from jax import lax
from jax.experimental import pallas as pl
from jax.experimental.pallas import tpu as pltpu
from jax.sharding import PartitionSpec as P

MESH = pl.DeviceIdType.MESH
bf16 = jnp.bfloat16
f32 = jnp.float32
epsilon = 1e-06
root_half = 0.7978845608028654
cubic_coef = 0.044715

C = 128
ROWS = 32
COLS = 256
HID = 512
EXT = 22 * 16
VLIM = 60 * 1024 * 1024


def iota2(shape, dim):
    return lax.broadcasted_iota(jnp.int32, shape, dim)


def one_hot(hit):
    return jnp.where(hit, 1.0, 0.0).astype(bf16)


def place(rows, edges):
    o = iota2((rows, 1), 0)
    if edges:
        o = jnp.where(o >= 48, o + 256, o)
    return (o % 16) * 16 + o // 16 - 3


def swap(o):
    return (o % 16) * 16 + o // 16


def dot(a, b):
    return jnp.dot(a, b, preferred_element_type=f32)


def dot_t(a, b):
    return lax.dot_general(a, b, (((0,), (0,)), ((), ())), preferred_element_type=f32)


def conv_taps(ext, row, taps, k0, nk):
    acc = [None] * nk
    for a in range(7):
        win = [ext[row + a, k0 + kk] for kk in range(nk + 6)]
        w = [taps[a * 7 + b] for b in range(7)]
        for k in range(nk):
            p = win[k] * w[0]
            for b in range(1, 7):
                p = p + win[k + b] * w[b]
            p = p.astype(f32)
            acc[k] = p if acc[k] is None else acc[k] + p
    return acc


def gelu_parts(v):
    u = v * v
    t = jnp.tanh(v * (root_half + (root_half * cubic_coef) * u))
    h = 0.5 * t + 0.5
    act = v * h
    der = h + act * (1.0 - h) * (2.0 * root_half + (6.0 * root_half * cubic_coef) * u)
    return act, der


R = 2
M = R * COLS
NB = ROWS // R


def main_kernel(x, mask, cot, taps1, bias, gain, w_in, w_in_t, w_out, w_out_t,
                upd, back, edge, xp, gin, gout, small,
                ext, taps, perm, norm_s, unit_s, inv_s, up_s, mask_s, xs_s, hr, hc, send, recv):
    i = pl.program_id(0)

    @pl.when(i == 0)
    def _():
        exchange(x, x.at[:, pl.ds(0, 16)], x.at[:, pl.ds(COLS - 16, 16)], hr, hc, send, recv)
        for t in range(49):
            taps[t] = jnp.broadcast_to(taps1[t // 7, t % 7:t % 7 + 1], (16, C))
        col = iota2((1, COLS), 1)
        amat = one_hot(place(EXT, False) == col)
        h = iota2((1, 32), 1)
        bmat = one_hot(place(96, True) == jnp.where(h < 16, h - 16, 240 + h))
        perm[...] = one_hot(swap(iota2((COLS, 1), 0)) == col)

        def build(am, bm, main, side):
            full = dot(am, main)
            rim = dot(bm, side)
            return jnp.concatenate([full[:48] + rim[:48], full[48:304], full[304:] + rim[48:]], axis=0).astype(bf16)

        def inner(j, _):
            main = jnp.concatenate([x[2 * j], x[2 * j + 1]], axis=-1)
            side = jnp.concatenate([hc[2 * j + 3], hc[2 * j + 4]], axis=-1)
            full = build(amat, bmat, main, side)
            ext[2 * j + 3] = full[:, :C].reshape(22, 16, C)
            ext[2 * j + 4] = full[:, C:].reshape(22, 16, C)
            return 0

        lax.fori_loop(0, ROWS // 2, inner, 0)
        is_bottom = lax.axis_index("lat") == 0
        is_top = lax.axis_index("lat") == lax.axis_size("lat") - 1
        for e in range(3):
            main = jnp.where(is_bottom, jnp.zeros((COLS, C), bf16), hr[e])
            side = jnp.where(is_bottom, jnp.zeros((32, C), bf16), hc[e])
            ext[e] = build(amat, bmat, main, side).reshape(22, 16, C)
        acol = jnp.where(is_top, 255 - col, col)
        amat_t = one_hot(place(EXT, False) == acol)
        hpos = jnp.where(is_top, jnp.where(h < 16, -1 - h, 287 - h), jnp.where(h < 16, h - 16, 240 + h))
        bmat_t = one_hot(place(96, True) == hpos)
        for m in range(3):
            src = jnp.where(is_top, 2 - m, m)
            ext[35 + m] = build(amat_t, bmat_t, hr[3 + src], hc[35 + src]).reshape(22, 16, C)
        norm_s[...] = jnp.zeros_like(norm_s)
        unit_s[...] = jnp.zeros_like(unit_s)
        inv_s[...] = jnp.zeros_like(inv_s)
        up_s[...] = jnp.zeros_like(up_s)
        mask_s[...] = jnp.zeros_like(mask_s)
        xs_s[...] = jnp.zeros_like(xs_s)
        gin[...] = jnp.zeros_like(gin)
        gout[...] = jnp.zeros_like(gout)
        small[...] = jnp.zeros_like(small)

    other = 1 - i % 2
    slot = i % 2
    normed = norm_s[other]
    upstream = up_s[other]
    mixed = None
    bn = None
    for f in range(0, HID, 256):
        pre = dot(normed, w_in[:, f:f + 256])
        bh = dot(upstream, w_out_t[:, f:f + 256])
        act, der = gelu_parts(pre)
        hid = act.astype(bf16)
        bp = (bh * der).astype(bf16)
        mx = dot(hid, w_out[f:f + 256])
        bx = dot(bp, w_in_t[f:f + 256])
        mixed = mx if mixed is None else mixed + mx
        bn = bx if bn is None else bn + bx
        gin[:, f:f + 256] += dot_t(normed, bp)
        gout[:, f:f + 256] += dot_t(upstream, hid)
    mixed = (mixed * mask_s[other]).astype(bf16)
    pm = perm[...]
    unit = unit_s[other]
    bnf = bn.astype(bf16).astype(f32)
    g = bnf * gain[...]
    m1 = jnp.mean(g, axis=-1, keepdims=True)
    m2 = jnp.mean(g * unit, axis=-1, keepdims=True)
    bc = ((g - m1 - unit * m2) * inv_s[other]).astype(bf16)
    small[0:8] += jnp.sum((bnf * unit).reshape(M // 8, 8, C), axis=0)
    small[8:16] += jnp.sum(bc.astype(f32).reshape(M // 8, 8, C), axis=0)
    h32 = iota2((32, 1), 0)
    sel = one_hot(jnp.where(h32 < 16, h32, 224 + h32) == swap(iota2((1, COLS), 1)))
    for r in range(R):
        sl = slice(r * COLS, (r + 1) * COLS)
        nat = dot(pm, mixed[sl])
        upd[r] = (xs_s[other, sl].astype(f32) + nat).astype(bf16)
        back[r] = bc[sl]
        edge[r] = dot(sel, bc[sl]).astype(bf16)

    nb = jnp.minimum(i, NB - 1)
    ones = jnp.ones((COLS, C), bf16)
    for r in range(R):
        row = nb * R + r
        sl = slice(r * COLS, (r + 1) * COLS)
        accs = []
        for k0 in (0, 8):
            accs += conv_taps(ext, row, taps, k0, 8)
        conv = jnp.concatenate([a + bias[...] for a in accs], axis=0)
        centre = jnp.mean(conv, axis=-1, keepdims=True)
        shifted = conv - centre
        var = jnp.mean(shifted * shifted, axis=-1, keepdims=True)
        inv = lax.rsqrt(var + epsilon)
        unit = shifted * inv
        unit_s[slot, sl] = unit
        inv_s[slot, sl] = jnp.broadcast_to(inv, (COLS, C))
        norm_s[slot, sl] = (unit * gain[...]).astype(bf16)
        pmask = pm * mask[pl.ds(row, 1), :].astype(f32).astype(bf16)
        both = dot(pmask, jnp.concatenate([cot[r], ones], axis=-1))
        up_s[slot, sl] = both[:, :C].astype(bf16)
        mask_s[slot, sl] = both[:, C:]
        xs_s[slot, sl] = x[row]
        xp[r] = ext[row + 3, 3:19].reshape(COLS, C)


def main_call(x, mask, cot, depth_kernel, bias, gain, w_in, w_out):
    vm = pl.BlockSpec(memory_space=pltpu.VMEM)
    now = lambda i: (jnp.minimum(i, NB - 1), 0, 0)
    past = lambda i: (jnp.maximum(i - 1, 0), 0, 0)
    whole2 = lambda i: (0, 0)
    tile = jax.ShapeDtypeStruct((ROWS, COLS, C), bf16)
    return pl.pallas_call(
        main_kernel,
        grid=(NB + 1,),
        in_specs=[vm, vm, pl.BlockSpec((R, COLS, C), now), vm, vm, vm, vm, vm, vm, vm],
        out_specs=[pl.BlockSpec((R, COLS, C), past), pl.BlockSpec((R, COLS, C), past),
                   pl.BlockSpec((R, 32, C), past), pl.BlockSpec((R, COLS, C), now),
                   pl.BlockSpec((C, HID), whole2), pl.BlockSpec((C, HID), whole2), pl.BlockSpec((16, C), whole2)],
        out_shape=[tile, tile, jax.ShapeDtypeStruct((ROWS, 32, C), bf16), tile,
                   jax.ShapeDtypeStruct((C, HID), f32), jax.ShapeDtypeStruct((C, HID), f32),
                   jax.ShapeDtypeStruct((16, C), f32)],
        scratch_shapes=[
            pltpu.VMEM((38, 22, 16, C), bf16), pltpu.VMEM((49, 16, C), bf16), pltpu.VMEM((COLS, COLS), bf16),
            pltpu.VMEM((2, M, C), bf16), pltpu.VMEM((2, M, C), f32), pltpu.VMEM((2, M, C), f32),
            pltpu.VMEM((2, M, C), bf16), pltpu.VMEM((2, M, C), f32), pltpu.VMEM((2, M, C), bf16),
            pltpu.VMEM((6, COLS, C), bf16), pltpu.VMEM((ROWS + 6, 32, C), bf16),
            pltpu.SemaphoreType.DMA((8,)), pltpu.SemaphoreType.DMA((8,))],
        compiler_params=pltpu.CompilerParams(collective_id=0, has_side_effects=True, vmem_limit_bytes=VLIM),
        name="conv_norm_mlp",
    )(x, mask, cot, depth_kernel, bias.reshape(1, C), gain.reshape(1, C),
      w_in, w_in.T, w_out, w_out.T)


def back_kernel(back, edge, xp, cot, taps1, out, gk, ext, fold, taps, perm, gks, hr, hc, send, recv):
    i = pl.program_id(0)

    @pl.when(i == 0)
    def _():
        exchange(back, edge.at[:, pl.ds(0, 16)], edge.at[:, pl.ds(16, 16)], hr, hc, send, recv)
        for t in range(49):
            taps[t] = jnp.broadcast_to(taps1[t // 7, t % 7:t % 7 + 1], (16, C))
        for t in range(49):
            taps[49 + t] = taps[48 - t]
        col = swap(iota2((1, COLS), 1))
        place_e = place(96, True)
        amat = one_hot(place_e == col)
        h = iota2((1, 32), 1)
        bmat = one_hot(place_e == jnp.where(h < 16, h - 16, 240 + h))
        perm[...] = one_hot(swap(iota2((COLS, 1), 0)) == iota2((1, COLS), 1))
        gks[...] = jnp.zeros_like(gks)

        def put(dst, e, main, rim):
            rim = rim.astype(bf16).reshape(6, 16, C)
            dst[e, 3:19] = main.reshape(16, 16, C)
            dst[e, 0:3] = rim[0:3]
            dst[e, 19:22] = rim[3:6]

        def inner(j, _):
            b0 = back[2 * j]
            b1 = back[2 * j + 1]
            main = jnp.concatenate([b0, b1], axis=-1)
            side = jnp.concatenate([hc[2 * j + 3], hc[2 * j + 4]], axis=-1)
            rim = dot(amat, main) + dot(bmat, side)
            put(ext, 2 * j + 3, b0, rim[:, :C])
            put(ext, 2 * j + 4, b1, rim[:, C:])
            return 0

        lax.fori_loop(0, ROWS // 2, inner, 0)
        is_bottom = lax.axis_index("lat") == 0
        is_top = lax.axis_index("lat") == lax.axis_size("lat") - 1
        zero_m = jnp.zeros((COLS, C), bf16)
        zero_s = jnp.zeros((32, C), bf16)
        for e in range(3):
            main = jnp.where(is_bottom, zero_m, hr[e])
            put(ext, e, main, dot(amat, main) + dot(bmat, jnp.where(is_bottom, zero_s, hc[e])))
            main = jnp.where(is_top, zero_m, hr[3 + e])
            put(ext, 35 + e, main, dot(amat, main) + dot(bmat, jnp.where(is_top, zero_s, hc[35 + e])))
        amat_f = one_hot(place(EXT, False) == 255 - col)
        bmat_f = one_hot(place_e == jnp.where(h < 16, -1 - h, 287 - h))
        for m in range(3):
            full = dot(amat_f, hr[5 - m])
            rim = dot(bmat_f, hc[37 - m])
            full = jnp.concatenate([full[:48] + rim[:48], full[48:304], full[304:] + rim[48:]], axis=0).astype(bf16)
            fold[m] = jnp.where(is_top, full, jnp.zeros_like(full)).reshape(22, 16, C)

    def add_row(src, pairs, r, k0, nk, acc, tap0):
        xv = [xp[r, (k0 + k) * 16:(k0 + k + 1) * 16] for k in range(nk)]
        for row, a in pairs:
            win = [src[row, k0 + kk] for kk in range(nk + 6)]
            w = [taps[tap0 + a * 7 + b] for b in range(7)]
            for k in range(nk):
                p = win[k] * w[0]
                for b in range(1, 7):
                    p = p + win[k + b] * w[b]
                p = p.astype(f32)
                acc[k] = p if acc[k] is None else acc[k] + p
            for b in range(7):
                q = win[b] * xv[0]
                for k in range(1, nk):
                    q = q + win[k + b] * xv[k]
                t = a * 7 + b
                q = q.astype(f32)
                gks[(48 - t) if tap0 else t] += q[:8] + q[8:]

    for r in range(RB):
        row = i * RB + r
        accs = []
        for k0 in (0, 8):
            acc = [None] * 8
            add_row(ext, [(row + a, a) for a in range(7)], r, k0, 8, acc, 49)
            accs += acc
        conv = jnp.concatenate(accs, axis=0)
        out[r] = (cot[r].astype(f32) + dot(perm[...], conv.astype(bf16))).astype(bf16)

    @pl.when((i == ROWS // RB - 1) & (lax.axis_index("lat") == lax.axis_size("lat") - 1))
    def _():
        for t in range(3):
            r = RB - 3 + t
            accs = []
            for k0 in (0, 8):
                acc = [None] * 8
                add_row(fold, [(m, 6 - t + m) for m in range(t + 1)], r, k0, 8, acc, 0)
                accs += acc
            conv = jnp.concatenate(accs, axis=0)
            out[r] = (out[r].astype(f32) + dot(perm[...], conv.astype(bf16))).astype(bf16)

    @pl.when(i == ROWS // RB - 1)
    def _():
        gk[...] = jnp.zeros_like(gk)
        for t in range(49):
            gk[t:t + 1] = jnp.sum(gks[t], axis=0, keepdims=True)


RB = 4


def back_call(back, edge, xp, cot, depth_kernel):
    vm = pl.BlockSpec(memory_space=pltpu.VMEM)
    blk = pl.BlockSpec((RB, COLS, C), lambda i: (i, 0, 0))
    return pl.pallas_call(
        back_kernel,
        grid=(ROWS // RB,),
        in_specs=[vm, vm, blk, blk, vm],
        out_specs=[blk, pl.BlockSpec((64, C), lambda i: (0, 0))],
        out_shape=[jax.ShapeDtypeStruct((ROWS, COLS, C), bf16), jax.ShapeDtypeStruct((64, C), f32)],
        scratch_shapes=[
            pltpu.VMEM((38, 22, 16, C), bf16), pltpu.VMEM((3, 22, 16, C), bf16), pltpu.VMEM((98, 16, C), bf16),
            pltpu.VMEM((COLS, COLS), bf16), pltpu.VMEM((49, 8, C), f32),
            pltpu.VMEM((6, COLS, C), bf16), pltpu.VMEM((ROWS + 6, 32, C), bf16),
            pltpu.SemaphoreType.DMA((8,)), pltpu.SemaphoreType.DMA((8,))],
        compiler_params=pltpu.CompilerParams(collective_id=1, has_side_effects=True, vmem_limit_bytes=VLIM),
        name="conv_back",
    )(back, edge, xp, cot, depth_kernel)


def neighbours(lat, lon):
    nl = lax.axis_size("lon")
    top = lat == lax.axis_size("lat") - 1
    low = lat > 0
    left = lax.rem(lon + nl - 1, nl)
    right = lax.rem(lon + 1, nl)
    up = jnp.where(top, lat, lat + 1)
    down = jnp.where(low, lat - 1, lat)
    f0 = jnp.where(top, nl - 1 - lon, lon)
    fl = jnp.where(top, lax.rem(nl - lon, nl), left)
    fr = jnp.where(top, lax.rem(2 * nl - 2 - lon, nl), right)
    return top, low, up, down, left, right, f0, fl, fr


def exchange(rows, lcols, rcols, hr, hc, send, recv):
    lat = lax.axis_index("lat")
    lon = lax.axis_index("lon")
    top, low, up, down, left, right, f0, fl, fr = neighbours(lat, lon)
    far_l = jnp.logical_not(top & (fl == lon))
    far_r = jnp.logical_not(top & (fr == lon))
    inner = jnp.logical_not(top)

    def greet(a, b):
        pl.semaphore_signal(barrier, inc=1, device_id=(a, b), device_id_type=MESH)

    barrier = pltpu.get_barrier_semaphore()
    greet(lat, left)
    greet(lat, right)
    greet(up, f0)

    @pl.when(far_l)
    def _():
        greet(up, fl)

    @pl.when(far_r)
    def _():
        greet(up, fr)

    @pl.when(low)
    def _():
        greet(down, lon)
        greet(down, left)
        greet(down, right)

    count = 3 + jnp.where(far_l, 1, 0) + jnp.where(far_r, 1, 0) + jnp.where(low, 3, 0)
    pl.semaphore_wait(barrier, count)

    def copy(src, dst, s, slot, a, b):
        return pltpu.make_async_remote_copy(src_ref=src, dst_ref=dst, send_sem=send.at[s], recv_sem=recv.at[slot],
                                            device_id=(a, b), device_id_type=MESH)

    last = pl.ds(ROWS - 3, 3)
    first = pl.ds(0, 3)
    lo, mid, hi = pl.ds(0, 3), pl.ds(3, ROWS), pl.ds(ROWS + 3, 3)
    to_l, to_r = pl.ds(0, 16), pl.ds(16, 16)
    c_right = copy(rcols, hc.at[mid, to_l], 2, 2, lat, right)
    c_left = copy(lcols, hc.at[mid, to_r], 3, 3, lat, left)
    up_n = copy(rows.at[last], hr.at[pl.ds(0, 3)], 1, 0, up, f0)
    up_f = copy(rows.at[last], hr.at[pl.ds(3, 3)], 1, 1, up, f0)
    ul_n = copy(lcols.at[last], hc.at[lo, to_r], 6, 5, up, fl)
    ul_f = copy(lcols.at[last], hc.at[hi, to_l], 6, 6, up, fl)
    ur_n = copy(rcols.at[last], hc.at[lo, to_l], 7, 4, up, fr)
    ur_f = copy(rcols.at[last], hc.at[hi, to_r], 7, 7, up, fr)
    dn = copy(rows.at[first], hr.at[pl.ds(3, 3)], 0, 1, down, lon)
    dl = copy(lcols.at[first], hc.at[hi, to_r], 4, 7, down, left)
    dr = copy(rcols.at[first], hc.at[hi, to_l], 5, 6, down, right)
    own_l = pltpu.make_async_copy(lcols.at[last], hc.at[hi, to_l], send.at[6])
    own_r = pltpu.make_async_copy(rcols.at[last], hc.at[hi, to_r], send.at[7])

    @pl.when(inner)
    def _():
        up_n.start()
        ul_n.start()
        ur_n.start()

    @pl.when(top)
    def _():
        up_f.start()

    @pl.when(top & far_l)
    def _():
        ul_f.start()

    @pl.when(top & far_r)
    def _():
        ur_f.start()

    @pl.when(jnp.logical_not(far_l))
    def _():
        own_l.start()

    @pl.when(jnp.logical_not(far_r))
    def _():
        own_r.start()

    @pl.when(low)
    def _():
        dn.start()
        dl.start()
        dr.start()

    c_right.start()
    c_left.start()
    c_right.wait()
    c_left.wait()

    dn.wait_recv()

    @pl.when(far_l)
    def _():
        dr.wait_recv()

    @pl.when(far_r)
    def _():
        dl.wait_recv()

    @pl.when(jnp.logical_not(far_l))
    def _():
        own_l.wait()

    @pl.when(jnp.logical_not(far_r))
    def _():
        own_r.wait()

    @pl.when(low)
    def _():
        up_n.wait_recv()
        ul_n.wait_recv()
        ur_n.wait_recv()
        dn.wait_send()
        dl.wait_send()
        dr.wait_send()

    up_n.wait_send()

    @pl.when(far_l)
    def _():
        ul_n.wait_send()

    @pl.when(far_r)
    def _():
        ur_n.wait_send()


N_LON = 16
N_LAT = 8
SEG = 64


def sum_kernel(gin, gout, gk, small, scale, o_in, o_out, o_k, o_bias, o_gain, wb, sb, r1, r2, r3, c2, s1, q1, s2, q2, s3, q3):
    lat = lax.axis_index("lat")
    lon = lax.axis_index("lon")
    barrier = pltpu.get_barrier_semaphore()

    def greet_lon(d, _):
        pl.semaphore_signal(barrier, inc=1, device_id=(lat, lax.rem(lon + d, N_LON)), device_id_type=MESH)
        return 0

    def greet_lat(d, _):
        pl.semaphore_signal(barrier, inc=1, device_id=(lax.rem(lat + d, N_LAT), lon), device_id_type=MESH)
        return 0

    lax.fori_loop(1, N_LON, greet_lon, 0)
    lax.fori_loop(1, N_LAT, greet_lat, 0)
    rest = jnp.concatenate([gk[:49], jnp.sum(small[:8], axis=0, keepdims=True),
                            jnp.sum(small[8:], axis=0, keepdims=True), jnp.zeros((13, C), f32)], axis=0).astype(bf16)
    for c in range(N_LON):
        r0, c0 = c // 4 * 32, c % 4 * C
        wb[c, 0:32] = gin[r0:r0 + 32, c0:c0 + C].astype(bf16)
        wb[c, 32:SEG] = gout[r0:r0 + 32, c0:c0 + C].astype(bf16)
        wb[c, SEG:2 * SEG] = rest
    pl.semaphore_wait(barrier, N_LON + N_LAT - 2)

    def first(d):
        to = lax.rem(lon + d, N_LON)
        return pltpu.make_async_remote_copy(src_ref=wb.at[to], dst_ref=r1.at[d], send_sem=s1.at[d], recv_sem=q1.at[d],
                                            device_id=(lat, to), device_id_type=MESH)

    def second(d):
        return pltpu.make_async_remote_copy(src_ref=c2, dst_ref=r2.at[lat], send_sem=s2.at[d], recv_sem=q2.at[d],
                                            device_id=(lax.rem(lat + d, N_LAT), lon), device_id_type=MESH)

    def third(d):
        return pltpu.make_async_remote_copy(src_ref=sb, dst_ref=r3.at[lon], send_sem=s3.at[d], recv_sem=q3.at[d],
                                            device_id=(lat, lax.rem(lon + d, N_LON)), device_id_type=MESH)

    def run(make, n):
        def go(d, _):
            make(d).start()
            return 0

        lax.fori_loop(1, n, go, 0)

    def arrive(make, n):
        def go(d, _):
            make(d).wait()
            return 0

        lax.fori_loop(1, n, go, 0)

    run(first, N_LON)
    arrive(first, N_LON)
    total = wb[lon].astype(f32)
    for d in range(1, N_LON):
        total = total + r1[d].astype(f32)
    c2[...] = total.astype(bf16)
    run(second, N_LAT)
    r2[lat] = c2[...]
    arrive(second, N_LAT)
    total = r2[0].astype(f32)
    for d in range(1, N_LAT):
        total = total + r2[d].astype(f32)
    total = total * scale[0]
    sb[...] = total[:SEG].astype(bf16)
    run(third, N_LON)
    for a in range(7):
        o_k[a] = total[SEG + 7 * a:SEG + 7 * a + 7]
    o_gain[...] = total[SEG + 49:SEG + 50]
    o_bias[...] = total[SEG + 50:SEG + 51]
    r3[lon] = sb[...]
    arrive(third, N_LON)
    for j in range(4):
        for k in range(4):
            o_in[32 * k:32 * k + 32, j * C:(j + 1) * C] = r3[4 * k + j, 0:32].astype(f32)
        whole = jnp.concatenate([r3[4 * k + j, 32:SEG] for k in range(4)], axis=0).astype(f32)
        o_out[j * C:(j + 1) * C] = whole.T


def sum_call(gin, gout, gk, small, scale):
    vm = pl.BlockSpec(memory_space=pltpu.VMEM)
    dma = pltpu.SemaphoreType.DMA
    return pl.pallas_call(
        sum_kernel,
        in_specs=[vm, vm, vm, vm, pl.BlockSpec(memory_space=pltpu.SMEM)],
        out_specs=[vm] * 5,
        out_shape=[jax.ShapeDtypeStruct((C, HID), f32), jax.ShapeDtypeStruct((HID, C), f32),
                   jax.ShapeDtypeStruct((7, 7, C), f32), jax.ShapeDtypeStruct((1, C), f32), jax.ShapeDtypeStruct((1, C), f32)],
        scratch_shapes=[
            pltpu.VMEM((N_LON, 2 * SEG, C), bf16), pltpu.VMEM((SEG, C), bf16),
            pltpu.VMEM((N_LON, 2 * SEG, C), bf16), pltpu.VMEM((N_LAT, 2 * SEG, C), bf16), pltpu.VMEM((N_LON, SEG, C), bf16),
            pltpu.VMEM((2 * SEG, C), bf16),
            dma((N_LON,)), dma((N_LON,)), dma((N_LAT,)), dma((N_LAT,)), dma((N_LON,)), dma((N_LON,))],
        compiler_params=pltpu.CompilerParams(collective_id=2, has_side_effects=True, vmem_limit_bytes=VLIM),
        name="sum_grads",
    )(gin, gout, gk, small, scale)


def body(ocean_state, sea_mask, depth_kernel, conv_bias, norm_gain, w_in, w_out, cotangent):
    upd, back, edge, xp, gin, gout, small = main_call(
        ocean_state, sea_mask, cotangent, depth_kernel, conv_bias, norm_gain, w_in, w_out)
    grad_state, gk = back_call(back, edge, xp, cotangent, depth_kernel)
    cells = COLS * ROWS * lax.axis_size("lat") * lax.axis_size("lon")
    scale = 1.0 / jnp.sqrt(jnp.full((1,), cells, f32))
    o_in, o_out, o_k, o_bias, o_gain = sum_call(gin, gout, gk, small, scale)
    return upd, grad_state, o_k, o_bias.reshape(C), o_gain.reshape(C), o_in, o_out


def solution(mesh):
    tile = P("lat", "lon", None)
    return jax.shard_map(
        body,
        mesh=mesh,
        in_specs=(tile, P("lat", "lon"), P(), P(), P(), P(), P(), tile),
        out_specs=(tile, tile, P(), P(), P(), P(), P()),
        check_vma=False,
    )
```

```python
import functools
import jax
import jax.numpy as jnp
from jax import lax
from jax.experimental import pallas as pl
from jax.experimental.pallas import tpu as pltpu
from jax.sharding import PartitionSpec as P

MESH = pl.DeviceIdType.MESH
bf16 = jnp.bfloat16
f32 = jnp.float32
epsilon = 1e-06
root_half = 0.7978845608028654
cubic_coef = 0.044715

C = 128
ROWS = 32
COLS = 256
HID = 512
EXT = 22 * 16
N_LON = 16
N_LAT = 8
SEG = 64
R = 2
M = R * COLS
NB = ROWS // R
FIRST = 7
CHUNKS = (3, 3, 4, 4, 5, 5)
VLIM = 60 * 1024 * 1024


def iota2(shape, dim):
    return lax.broadcasted_iota(jnp.int32, shape, dim)


def one_hot(hit):
    return jnp.where(hit, 1.0, 0.0).astype(bf16)


def swap(o):
    return (o % 16) * 16 + o // 16


def rim_place():
    o = iota2((96, 1), 0)
    o = jnp.where(o >= 48, o + 256, o)
    return (o % 16) * 16 + o // 16 - 3


def dot(a, b):
    return jnp.dot(a, b, preferred_element_type=f32)


def dot_t(a, b):
    return lax.dot_general(a, b, (((0,), (0,)), ((), ())), preferred_element_type=f32)


def conv_part(ext, row, wmat, flip, lo, hi):
    parts = []
    for u in range(lo, hi):
        j, b = u // 7, u % 7
        e = row + 2 * (3 - j if flip else j)
        s = 6 - b if flip else b
        pair = [ext[e, s:s + 16].reshape(COLS, C), ext[e + 1, s:s + 16].reshape(COLS, C)]
        parts += pair[::-1] if flip else pair
    return dot(jnp.concatenate(parts, axis=-1), wmat[lo * 256:hi * 256])


def gelu_parts(v):
    u = v * v
    t = jnp.tanh(v * (root_half + (root_half * cubic_coef) * u))
    h = 0.5 * t + 0.5
    act = v * h
    der = h + act * (1.0 - h) * (2.0 * root_half + (6.0 * root_half * cubic_coef) * u)
    return act, der


def main_block(n):
    late = n - FIRST
    edge = jnp.where(late < 2, late, late + 12)
    return jnp.where(n < FIRST, n + 2, jnp.where(late < 4, edge, n - 2))


def back_block(n):
    late = n - 12
    return jnp.where(n < 12, n + 2, jnp.where(late < 2, late, late + 12))


class Links:
    def __init__(self):
        self.lat = lax.axis_index("lat")
        self.lon = lax.axis_index("lon")
        lat, lon = self.lat, self.lon
        self.top = lat == N_LAT - 1
        self.low = lat > 0
        self.inner = jnp.logical_not(self.top)
        self.left = lax.rem(lon + N_LON - 1, N_LON)
        self.right = lax.rem(lon + 1, N_LON)
        self.up = jnp.where(self.top, lat, lat + 1)
        self.down = jnp.where(self.low, lat - 1, lat)
        self.f0 = jnp.where(self.top, N_LON - 1 - lon, lon)
        self.fl = jnp.where(self.top, lax.rem(N_LON - lon, N_LON), self.left)
        self.fr = jnp.where(self.top, lax.rem(2 * N_LON - 2 - lon, N_LON), self.right)
        self.far_l = jnp.logical_not(self.top & (self.fl == lon))
        self.far_r = jnp.logical_not(self.top & (self.fr == lon))

    def greet(self):
        barrier = pltpu.get_barrier_semaphore()

        def signal(a, b):
            pl.semaphore_signal(barrier, inc=1, device_id=(a, b), device_id_type=MESH)

        def along_lon(d, _):
            signal(self.lat, lax.rem(self.lon + d, N_LON))
            return 0

        def along_lat(d, _):
            signal(lax.rem(self.lat + d, N_LAT), self.lon)
            return 0

        lax.fori_loop(1, N_LON, along_lon, 0)
        lax.fori_loop(1, N_LAT, along_lat, 0)

        @pl.when(self.inner)
        def _():
            signal(self.up, self.left)
            signal(self.up, self.right)

        @pl.when(self.low)
        def _():
            signal(self.down, self.left)
            signal(self.down, self.right)

    def met(self):
        count = N_LON + N_LAT - 2 + jnp.where(self.inner, 2, 0) + jnp.where(self.low, 2, 0)
        pl.semaphore_wait(pltpu.get_barrier_semaphore(), count)


def copy(src, dst, send, recv, a, b):
    return pltpu.make_async_remote_copy(src_ref=src, dst_ref=dst, send_sem=send, recv_sem=recv,
                                        device_id=(a, b), device_id_type=MESH)


def when(cond, todo):
    @pl.when(cond)
    def _():
        todo()


class ColumnExchange:
    def __init__(self, lk, lcols, rcols, hc, rows, send, recv, base):
        to_l, to_r = pl.ds(0, 16), pl.ds(16, 16)
        self.copies = []
        for k, (start, n) in enumerate(rows):
            own, dst = pl.ds(start, n), pl.ds(start + 3, n)
            s = base + 2 * k
            self.copies += [copy(rcols.at[own], hc.at[dst, to_l], send.at[s], recv.at[s], lk.lat, lk.right),
                            copy(lcols.at[own], hc.at[dst, to_r], send.at[s + 1], recv.at[s + 1], lk.lat, lk.left)]

    def start(self):
        for c in self.copies:
            c.start()

    def wait(self):
        for c in self.copies:
            c.wait()


class RowExchange:
    def __init__(self, lk, first, last, to_lo, to_hi, to_fold, lcols, rcols, hc, send, recv):
        self.lk = lk
        lo, hi = pl.ds(0, 3), pl.ds(ROWS + 3, 3)
        to_l, to_r = pl.ds(0, 16), pl.ds(16, 16)
        l_first, l_last = lcols.at[pl.ds(0, 3)], lcols.at[pl.ds(ROWS - 3, 3)]
        r_first, r_last = rcols.at[pl.ds(0, 3)], rcols.at[pl.ds(ROWS - 3, 3)]
        self.up_n = copy(last, to_lo, send.at[1], recv.at[0], lk.up, lk.f0)
        self.up_f = copy(last, to_fold, send.at[1], recv.at[1], lk.up, lk.f0)
        self.ul_n = copy(l_last, hc.at[lo, to_r], send.at[4], recv.at[3], lk.up, lk.fl)
        self.ul_f = copy(l_last, hc.at[hi, to_l], send.at[4], recv.at[4], lk.up, lk.fl)
        self.ur_n = copy(r_last, hc.at[lo, to_l], send.at[5], recv.at[2], lk.up, lk.fr)
        self.ur_f = copy(r_last, hc.at[hi, to_r], send.at[5], recv.at[5], lk.up, lk.fr)
        self.dn = copy(first, to_hi, send.at[0], recv.at[1], lk.down, lk.lon)
        self.dl = copy(l_first, hc.at[hi, to_r], send.at[2], recv.at[5], lk.down, lk.left)
        self.dr = copy(r_first, hc.at[hi, to_l], send.at[3], recv.at[4], lk.down, lk.right)
        self.own_l = pltpu.make_async_copy(l_last, hc.at[hi, to_l], send.at[4])
        self.own_r = pltpu.make_async_copy(r_last, hc.at[hi, to_r], send.at[5])

    def start(self):
        lk = self.lk

        def inner():
            self.ul_n.start()
            self.ur_n.start()
            self.up_n.start()

        def low():
            self.dl.start()
            self.dr.start()
            self.dn.start()

        when(lk.inner, inner)
        when(lk.top & lk.far_l, self.ul_f.start)
        when(lk.top & lk.far_r, self.ur_f.start)
        when(jnp.logical_not(lk.far_l), self.own_l.start)
        when(jnp.logical_not(lk.far_r), self.own_r.start)
        when(lk.top, self.up_f.start)
        when(lk.low, low)

    def wait(self):
        lk = self.lk

        def low():
            self.up_n.wait_recv()
            self.ul_n.wait_recv()
            self.ur_n.wait_recv()
            self.dn.wait_send()
            self.dl.wait_send()
            self.dr.wait_send()

        when(lk.inner, self.dn.wait_recv)
        when(lk.top, self.up_f.wait_recv)
        when(lk.far_l, self.dr.wait_recv)
        when(lk.far_r, self.dl.wait_recv)
        when(jnp.logical_not(lk.far_l), self.own_l.wait)
        when(jnp.logical_not(lk.far_r), self.own_r.wait)
        when(lk.low, low)
        self.up_n.wait_send()
        when(lk.far_l, self.ul_n.wait_send)
        when(lk.far_r, self.ur_n.wait_send)


def fan(make, n, wait):
    def go(d, _):
        if wait:
            make(d).wait()
        else:
            make(d).start()
        return 0

    lax.fori_loop(1, n, go, 0)


def kernel(x, mask, cot_hbm, taps1, bias, gain, w_in, w_out, scale,
           upd_hbm, out_hbm, o_in, o_out, o_k, o_bias, o_gain,
           cot, upd, out, ext, ext2, wmat, taps, perm, rim_a, rim_b, w_in_t, w_out_t,
           raw_s, edge, hr, hc, hr2, hc2, fold, gin, gout, gks, small,
           wb, c1, c2, c3, r1, r2, r3, q1, q2,
           io, cs, cr, rs, rr, cs2, cr2, rs2, rr2, a1, b1, a2, b2, a3, b3, a4, b4, a5, b5):
    lk = Links()
    lat, lon = lk.lat, lk.lon
    for cond, e0 in ((jnp.logical_not(lk.low), 0), (lk.top, ROWS + 3)):
        @pl.when(cond)
        def _():
            for e in range(3):
                ext2[e0 + e] = jnp.zeros((22, 16, C), bf16)

    lk.greet()
    cot_in = pltpu.make_async_copy(cot_hbm, cot, io.at[0])
    cot_in.start()

    lane = iota2((1, COLS), 1)
    h32 = iota2((1, 32), 1)
    perm[...] = one_hot(swap(iota2((COLS, 1), 0)) == lane)
    place = rim_place()
    rim_a[...] = one_hot(place == lane)
    rim_b[...] = one_hot(place == jnp.where(h32 < 16, h32 - 16, 240 + h32))

    cols1 = ColumnExchange(lk, x.at[:, pl.ds(0, 16)], x.at[:, pl.ds(COLS - 16, 16)], hc, [(0, ROWS)], cs, cr, 0)
    rows1 = RowExchange(lk, x.at[pl.ds(0, 3)], x.at[pl.ds(ROWS - 3, 3)], hr.at[pl.ds(0, 3)], hr.at[pl.ds(3, 3)],
                        hr.at[pl.ds(3, 3)], x.at[:, pl.ds(0, 16)], x.at[:, pl.ds(COLS - 16, 16)], hc, rs, rr)
    lk.met()
    cols1.start()
    rows1.start()

    for t in range(49):
        taps[t] = jnp.broadcast_to(taps1[t // 7, t % 7:t % 7 + 1], (16, C))
    eye = one_hot(iota2((C, 1), 0) == iota2((1, C), 1))
    zero = jnp.zeros((C, C), bf16)
    for j in range(4):
        for b in range(7):
            for i in range(2):
                for o in range(2):
                    a = 2 * j + i - o
                    blk = eye * taps1[a, b:b + 1] if 0 <= a < 7 else zero
                    r0 = (j * 7 + b) * 256 + i * C
                    wmat[r0:r0 + C, o * C:(o + 1) * C] = blk
    w_in_t[...] = w_in[...].T
    w_out_t[...] = w_out[...].T
    for ref in (gin, gout, small, gks):
        ref[...] = jnp.zeros_like(ref)

    def build(j, _):
        full = dot(perm[...], jnp.concatenate([x[2 * j], x[2 * j + 1]], axis=-1)).astype(bf16)
        ext[2 * j + 3, 3:19] = full[:, :C].reshape(16, 16, C)
        ext[2 * j + 4, 3:19] = full[:, C:].reshape(16, 16, C)
        return 0

    lax.fori_loop(0, NB, build, 0)

    def put_rim(dst, e, rim):
        rim = rim.astype(bf16).reshape(6, 16, C)
        dst[e, 0:3] = rim[0:3]
        dst[e, 19:22] = rim[3:6]

    def rims1(j, _):
        main = jnp.concatenate([x[2 * j], x[2 * j + 1]], axis=-1)
        side = jnp.concatenate([hc[2 * j + 3], hc[2 * j + 4]], axis=-1)
        rim = dot(rim_a[...], main) + dot(rim_b[...], side)
        put_rim(ext, 2 * j + 3, rim[:, :C])
        put_rim(ext, 2 * j + 4, rim[:, C:])
        return 0

    cols1.wait()
    lax.fori_loop(0, NB, rims1, 0)
    cot_in.wait()

    def edges1():
        rows1.wait()
        zero_m = jnp.zeros((COLS, C), bf16)
        zero_s = jnp.zeros((32, C), bf16)
        for e in range(3):
            main = jnp.where(lk.low, hr[e], zero_m)
            side = jnp.where(lk.low, hc[e], zero_s)
            ext[e, 3:19] = dot(perm[...], main).astype(bf16).reshape(16, 16, C)
            put_rim(ext, e, dot(rim_a[...], main) + dot(rim_b[...], side))
        where = jnp.where(lk.top, 255 - lane, lane)
        own = one_hot(swap(iota2((COLS, 1), 0)) == where)
        ra = one_hot(place == where)
        side_col = jnp.where(lk.top, jnp.where(h32 < 16, -1 - h32, 287 - h32), jnp.where(h32 < 16, h32 - 16, 240 + h32))
        rb = one_hot(place == side_col)
        for m in range(3):
            src = jnp.where(lk.top, 2 - m, m)
            main = hr[3 + src]
            ext[35 + m, 3:19] = dot(own, main).astype(bf16).reshape(16, 16, C)
            put_rim(ext, 35 + m, dot(ra, main) + dot(rb, hc[35 + src]))

    cut = [(0, 18), (28, 4)]
    l_edge, r_edge = edge.at[:, pl.ds(0, 16)], edge.at[:, pl.ds(16, 16)]
    cols2a = ColumnExchange(lk, l_edge, r_edge, hc2, cut, cs2, cr2, 0)
    cols2b = ColumnExchange(lk, l_edge, r_edge, hc2, [(18, 10)], cs2, cr2, 4)
    rows2 = RowExchange(lk, ext2.at[pl.ds(3, 3), pl.ds(3, 16)], ext2.at[pl.ds(ROWS, 3), pl.ds(3, 16)],
                        ext2.at[pl.ds(0, 3), pl.ds(3, 16)], ext2.at[pl.ds(ROWS + 3, 3), pl.ds(3, 16)], hr2,
                        l_edge, r_edge, hc2, rs2, rr2)

    def sends2():
        cols2a.start()
        rows2.start()

    ones = jnp.ones((COLS, C), bf16)

    hs = iota2((32, 1), 0)
    sel = one_hot(jnp.where(hs < 16, hs, 224 + hs) == swap(lane))

    def block_work(new, old, slot):
        state = [None, 0]

        def conv(n):
            lo = state[1]
            part = conv_part(ext, new * R, wmat, False, lo, lo + n)
            state[0] = part if lo == 0 else state[0] + part
            state[1] = lo + n

        units, invs, norms, ups, masks = [], [], [], [], []
        for r in range(R):
            row = old * R + r
            raw = raw_s[1 - slot, :, r * C:(r + 1) * C] + bias[...]
            centre = jnp.mean(raw, axis=-1, keepdims=True)
            shifted = raw - centre
            var = jnp.mean(shifted * shifted, axis=-1, keepdims=True)
            inv = lax.rsqrt(var + epsilon)
            unit = shifted * inv
            units.append(unit)
            invs.append(inv)
            norms.append((unit * gain[...]).astype(bf16))
            pmask = perm[...] * mask[pl.ds(row, 1), :].astype(f32).astype(bf16)
            pair = dot(pmask, jnp.concatenate([cot[row], ones], axis=-1))
            ups.append(pair[:, :C].astype(bf16))
            masks.append(pair[:, C:])
            conv(CHUNKS[r])
        jobs = [(r, f) for r in range(R) for f in range(0, HID, 256)]

        def first(job):
            r, f = job
            return dot(norms[r], w_in[:, f:f + 256]), dot(ups[r], w_out_t[:, f:f + 256])

        mixed, bn = [None] * R, [None] * R
        ready = first(jobs[0])
        for q, (r, f) in enumerate(jobs):
            pre, bh = ready
            conv(CHUNKS[R + q])
            if q + 1 < len(jobs):
                ready = first(jobs[q + 1])
            act, der = gelu_parts(pre)
            hid = act.astype(bf16)
            bp = (bh * der).astype(bf16)
            mx = dot(hid, w_out[f:f + 256])
            bx = dot(bp, w_in_t[f:f + 256])
            mixed[r] = mx if mixed[r] is None else mixed[r] + mx
            bn[r] = bx if bn[r] is None else bn[r] + bx
            gin[:, f:f + 256] += dot_t(norms[r], bp)
            gout[:, f:f + 256] += dot_t(ups[r], hid)
        conv(28 - state[1])
        raw_s[slot] = state[0]
        bcs = []
        for r in range(R):
            unit = units[r]
            bnf = bn[r].astype(bf16).astype(f32)
            g = bnf * gain[...]
            m1 = jnp.mean(g, axis=-1, keepdims=True)
            m2 = jnp.mean(g * unit, axis=-1, keepdims=True)
            bc = ((g - m1 - unit * m2) * invs[r]).astype(bf16)
            small[0:8] += jnp.sum((bnf * unit).reshape(COLS // 8, 8, C), axis=0)
            small[8:16] += jnp.sum(bc.astype(f32).reshape(COLS // 8, 8, C), axis=0)
            ext2[old * R + r + 3, 3:19] = bc.reshape(16, 16, C)
            bcs.append(bc)
        nat = dot(perm[...], jnp.concatenate([(mixed[r] * masks[r]).astype(bf16) for r in range(R)], axis=-1))
        ends = dot(sel, jnp.concatenate(bcs, axis=-1)).astype(bf16)
        for r in range(R):
            row = old * R + r
            upd[row] = (x[row].astype(f32) + nat[:, r * C:(r + 1) * C]).astype(bf16)
            edge[row] = ends[:, r * C:(r + 1) * C]

    def main_step(n, _):
        when(n == FIRST, edges1)
        when(n == FIRST + 5, sends2)
        block_work(main_block(jnp.minimum(n, NB - 1)), main_block(jnp.maximum(n - 1, 0)), n % 2)
        return 0

    raw_s[0] = conv_part(ext, main_block(0) * R, wmat, False, 0, 28)
    lax.fori_loop(1, NB + 1, main_step, 0)

    upd_out = pltpu.make_async_copy(upd, upd_hbm, io.at[1])
    upd_out.start()
    cols2b.start()

    def hop1(d):
        to = lax.rem(lon + d, N_LON)
        return copy(wb.at[to], r1.at[d], a1.at[d], b1.at[d], lat, to)

    def hop2(d):
        return copy(c1, r2.at[lat], a2.at[d], b2.at[d], lax.rem(lat + d, N_LAT), lon)

    def hop3(d):
        return copy(c2, r3.at[lon], a3.at[d], b3.at[d], lat, lax.rem(lon + d, N_LON))

    def hop4(d):
        return copy(c3, q1.at[lon], a4.at[d], b4.at[d], lat, lax.rem(lon + d, N_LON))

    def hop5(d):
        return copy(c3, q2.at[lat], a5.at[d], b5.at[d], lax.rem(lat + d, N_LAT), lon)

    for c in range(N_LON):
        r0, c0 = c // 4 * 32, c % 4 * C
        wb[c, 0:32] = gin[r0:r0 + 32, c0:c0 + C].astype(bf16)
        wb[c, 32:SEG] = gout[r0:r0 + 32, c0:c0 + C].astype(bf16)
    fan(hop1, N_LON, False)

    def w_second():
        fan(hop1, N_LON, True)
        total = wb[lon].astype(f32)
        for d in range(1, N_LON):
            total = total + r1[d].astype(f32)
        c1[...] = total.astype(bf16)
        r2[lat] = c1[...]
        fan(hop2, N_LAT, False)

    def w_third():
        fan(hop2, N_LAT, True)
        total = r2[0].astype(f32)
        for d in range(1, N_LAT):
            total = total + r2[d].astype(f32)
        c2[...] = (total * scale[0]).astype(bf16)
        r3[lon] = c2[...]
        fan(hop3, N_LON, False)

    def rim2(e, row):
        main = ext2[e, 3:19].reshape(COLS, C)
        ra = one_hot(place == swap(lane))
        put_rim(ext2, e, dot(ra, main) + dot(rim_b[...], hc2[e]))

    def rims2(j, _):
        ra = one_hot(place == swap(lane))
        main = jnp.concatenate([ext2[2 * j + 3, 3:19].reshape(COLS, C), ext2[2 * j + 4, 3:19].reshape(COLS, C)], axis=-1)
        side = jnp.concatenate([hc2[2 * j + 3], hc2[2 * j + 4]], axis=-1)
        rim = dot(ra, main) + dot(rim_b[...], side)
        put_rim(ext2, 2 * j + 3, rim[:, :C])
        put_rim(ext2, 2 * j + 4, rim[:, C:])
        return 0

    cols2a.wait()
    lax.fori_loop(0, 9, rims2, 0)
    lax.fori_loop(14, 16, rims2, 0)

    def late_cols():
        cols2b.wait()
        lax.fori_loop(9, 14, rims2, 0)

    def edges2():
        rows2.wait()
        ra = one_hot(place == swap(lane))

        def rim(e):
            put_rim(ext2, e, dot(ra, ext2[e, 3:19].reshape(COLS, C)) + dot(rim_b[...], hc2[e]))

        def low():
            for e in range(3):
                rim(e)

        def inner():
            for e in range(3):
                rim(35 + e)

        def top():
            own = one_hot(swap(iota2((COLS, 1), 0)) == 255 - swap(lane))
            fa = one_hot(place == 255 - swap(lane))
            fb = one_hot(place == jnp.where(h32 < 16, -1 - h32, 287 - h32))
            for m in range(3):
                main = hr2[2 - m].reshape(COLS, C)
                fold[m, 3:19] = dot(own, main).astype(bf16).reshape(16, 16, C)
                put_rim(fold, m, dot(fa, main) + dot(fb, hc2[37 - m]))

        when(lk.low, low)
        when(lk.inner, inner)
        when(lk.top, top)

    def tap_sums(src, e, row, a, flip):
        for b in range(7):
            total = None
            for k0 in (0, 8):
                q = src[e, k0 + b] * ext[row + 3, 3 + k0]
                for k in range(k0 + 1, k0 + 8):
                    q = q + src[e, k + b] * ext[row + 3, 3 + k]
                total = q if total is None else total + q
            q = total.astype(f32)
            t = a * 7 + b
            gks[(48 - t) if flip else t] += q[:8] + q[8:]

    def back_step(n, _):
        when(n == 5, late_cols)
        when(n == 6, w_second)
        when(n == 11, w_third)
        when(n == 12, edges2)
        row = back_block(n) * R
        conv = None
        for j in range(4):
            part = conv_part(ext2, row, wmat, True, 7 * j, 7 * j + 7)
            conv = part if conv is None else conv + part
            if j == 3:
                nat = dot(perm[...], conv.astype(bf16))
            for t in range((7 * j + 1) // 2, (7 * j + 8) // 2):
                tap_sums(ext2, row + t // 7 + t % 7, row + t // 7, t % 7, True)
        for r in range(R):
            out[row + r] = (cot[row + r].astype(f32) + nat[:, (1 - r) * C:(2 - r) * C]).astype(bf16)
        return 0

    lax.fori_loop(0, NB, back_step, 0)

    @pl.when(lk.top)
    def _():
        for t in range(3):
            row = ROWS - 3 + t
            acc = [None] * 16
            for m in range(t + 1):
                a = 6 - t + m
                for k in range(16):
                    p = fold[m, k] * taps[a * 7]
                    for b in range(1, 7):
                        p = p + fold[m, k + b] * taps[a * 7 + b]
                    p = p.astype(f32)
                    acc[k] = p if acc[k] is None else acc[k] + p
                tap_sums(fold, m, row, a, False)
            more = dot(perm[...], jnp.concatenate(acc, axis=0).astype(bf16))
            out[row] = (out[row].astype(f32) + more).astype(bf16)

    out_out = pltpu.make_async_copy(out, out_hbm, io.at[0])
    out_out.start()

    c3[...] = jnp.zeros_like(c3)
    rest = [jnp.sum(gks[t], axis=0, keepdims=True) for t in range(49)]
    rest += [jnp.sum(small[:8], axis=0, keepdims=True), jnp.sum(small[8:], axis=0, keepdims=True), jnp.zeros((13, C), f32)]
    c3[...] = jnp.concatenate(rest, axis=0).astype(bf16)
    fan(hop4, N_LON, False)
    q1[lon] = c3[...]
    fan(hop3, N_LON, True)
    for j in range(4):
        for k in range(4):
            o_in[32 * k:32 * k + 32, j * C:(j + 1) * C] = r3[4 * k + j, 0:32].astype(f32)
        whole = jnp.concatenate([r3[4 * k + j, 32:SEG] for k in range(4)], axis=0).astype(f32)
        o_out[j * C:(j + 1) * C] = whole.T
    fan(hop4, N_LON, True)
    total = q1[0].astype(f32)
    for d in range(1, N_LON):
        total = total + q1[d].astype(f32)
    c3[...] = total.astype(bf16)
    fan(hop5, N_LAT, False)
    q2[lat] = c3[...]
    fan(hop5, N_LAT, True)
    total = q2[0].astype(f32)
    for d in range(1, N_LAT):
        total = total + q2[d].astype(f32)
    total = total * scale[0]
    for a in range(7):
        o_k[a] = total[7 * a:7 * a + 7]
    o_gain[...] = total[49:50]
    o_bias[...] = total[50:51]
    upd_out.wait()
    out_out.wait()


def body(ocean_state, sea_mask, depth_kernel, conv_bias, norm_gain, w_in, w_out, cotangent):
    cells = COLS * ROWS * lax.axis_size("lat") * lax.axis_size("lon")
    scale = 1.0 / jnp.sqrt(jnp.full((1,), cells, f32))
    vm = pl.BlockSpec(memory_space=pltpu.VMEM)
    hbm = pl.BlockSpec(memory_space=pl.ANY)
    dma = pltpu.SemaphoreType.DMA
    V = pltpu.VMEM
    tile = jax.ShapeDtypeStruct((ROWS, COLS, C), bf16)
    upd, grad_state, o_in, o_out, o_k, o_bias, o_gain = pl.pallas_call(
        kernel,
        in_specs=[vm, vm, hbm, vm, vm, vm, vm, vm, pl.BlockSpec(memory_space=pltpu.SMEM)],
        out_specs=[hbm, hbm] + [vm] * 5,
        out_shape=[tile, tile, jax.ShapeDtypeStruct((C, HID), f32), jax.ShapeDtypeStruct((HID, C), f32),
                   jax.ShapeDtypeStruct((7, 7, C), f32), jax.ShapeDtypeStruct((1, C), f32), jax.ShapeDtypeStruct((1, C), f32)],
        scratch_shapes=[
            V((ROWS, COLS, C), bf16), V((ROWS, COLS, C), bf16), V((ROWS, COLS, C), bf16),
            V((38, 22, 16, C), bf16), V((38, 22, 16, C), bf16), V((28 * 256, 256), bf16), V((49, 16, C), bf16),
            V((COLS, COLS), bf16), V((96, COLS), bf16), V((96, 32), bf16), V((HID, C), bf16), V((C, HID), bf16),
            V((2, COLS, R * C), f32),
            V((ROWS, 32, C), bf16), V((6, COLS, C), bf16), V((ROWS + 6, 32, C), bf16),
            V((3, 16, 16, C), bf16), V((ROWS + 6, 32, C), bf16), V((3, 22, 16, C), bf16),
            V((C, HID), f32), V((C, HID), f32), V((49, 8, C), f32), V((16, C), f32),
            V((N_LON, SEG, C), bf16), V((SEG, C), bf16), V((SEG, C), bf16), V((SEG, C), bf16),
            V((N_LON, SEG, C), bf16), V((N_LAT, SEG, C), bf16), V((N_LON, SEG, C), bf16),
            V((N_LON, SEG, C), bf16), V((N_LAT, SEG, C), bf16),
            dma((2,)), dma((2,)), dma((2,)), dma((6,)), dma((6,)), dma((6,)), dma((6,)), dma((6,)), dma((6,)),
            dma((N_LON,)), dma((N_LON,)), dma((N_LAT,)), dma((N_LAT,)), dma((N_LON,)), dma((N_LON,)),
            dma((N_LON,)), dma((N_LON,)), dma((N_LAT,)), dma((N_LAT,))],
        compiler_params=pltpu.CompilerParams(collective_id=0, has_side_effects=True, vmem_limit_bytes=VLIM),
        name="block_step",
    )(ocean_state, sea_mask, cotangent, depth_kernel, conv_bias.reshape(1, C), norm_gain.reshape(1, C), w_in, w_out, scale)
    return upd, grad_state, o_k, o_bias.reshape(C), o_gain.reshape(C), o_in, o_out


def solution(mesh):
    tile = P("lat", "lon", None)
    return jax.shard_map(
        body,
        mesh=mesh,
        in_specs=(tile, P("lat", "lon"), P(), P(), P(), P(), P(), tile),
        out_specs=(tile, tile, P(), P(), P(), P(), P()),
        check_vma=False,
    )
```

```python
import functools
import jax
import jax.numpy as jnp
from jax import lax
from jax.experimental import pallas as pl
from jax.experimental.pallas import tpu as pltpu
from jax.sharding import PartitionSpec as P

MESH = pl.DeviceIdType.MESH
bf16 = jnp.bfloat16
f32 = jnp.float32
epsilon = 1e-06
root_half = 0.7978845608028654
cubic_coef = 0.044715
z_one = -2.0 * root_half * 1.4426950408889634
z_three = -2.0 * root_half * cubic_coef * 1.4426950408889634

C = 128
ROWS = 32
COLS = 256
HID = 512
EXT = 22 * 16
N_LON = 16
N_LAT = 8
SEG = 64
R = 4
NB = ROWS // R
FIRST = 3
MX_TAPS = 14
VLIM = 60 * 1024 * 1024


def iota2(shape, dim):
    return lax.broadcasted_iota(jnp.int32, shape, dim)


def one_hot(hit):
    return jnp.where(hit, 1.0, 0.0).astype(bf16)


def swap(o):
    return (o % 16) * 16 + o // 16


def rim_place():
    o = iota2((96, 1), 0)
    o = jnp.where(o >= 48, o + 256, o)
    return (o % 16) * 16 + o // 16 - 3


def dot(a, b):
    return jnp.dot(a, b, preferred_element_type=f32)


def dot_t(a, b):
    return lax.dot_general(a, b, (((0,), (0,)), ((), ())), preferred_element_type=f32)


def conv_part(ext, row, wmat, flip, lo, hi):
    sides = []
    for pair_row in (row, row + 2):
        parts = []
        for u in range(lo, hi):
            j, b = u // 7, u % 7
            e = pair_row + 2 * (3 - j if flip else j)
            s = 6 - b if flip else b
            pair = [ext[e, s:s + 16].reshape(COLS, C), ext[e + 1, s:s + 16].reshape(COLS, C)]
            parts += pair[::-1] if flip else pair
        sides.append(jnp.concatenate(parts, axis=-1))
    return dot(jnp.concatenate(sides, axis=0), wmat[lo * 256:hi * 256])


def conv_rest(ext, taps, row, o, k0, dst):
    acc = [None] * 8
    for a in range(MX_TAPS // 7 * 2 - o, 7):
        win = [ext[row + a, k0 + k] for k in range(14)]
        w = [taps[a * 7 + b] for b in range(7)]
        for k in range(8):
            p = win[k] * w[0]
            for b in range(1, 7):
                p = p + win[k + b] * w[b]
            p = p.astype(f32)
            acc[k] = p if acc[k] is None else acc[k] + p
    for k in range(8):
        dst[(k0 + k) * 16:(k0 + k + 1) * 16] = acc[k]


def conv_first(ext, taps, row, o):
    acc = [None] * 16
    for a in range(2 - o):
        w = [taps[48 - a * 7 - b] for b in range(7)]
        for k in range(16):
            p = ext[row + o + a, k] * w[0]
            for b in range(1, 7):
                p = p + ext[row + o + a, k + b] * w[b]
            p = p.astype(f32)
            acc[k] = p if acc[k] is None else acc[k] + p
    return jnp.concatenate(acc, axis=0)


def gelu_parts(v):
    u = v * v
    z = jnp.minimum(v * (z_one + z_three * u), 80.0)
    e = jnp.exp2(z)
    h = pl.reciprocal(e + 1.0, approx=True)
    act = v * h
    der = h + (act * (e * h)) * (2.0 * root_half + (6.0 * root_half * cubic_coef) * u)
    return act, der


def main_block(n):
    return jnp.where(n < FIRST, n + 1, jnp.where(n == FIRST, 0, jnp.where(n == FIRST + 1, NB - 1, n - 1)))


def back_block(n):
    return jnp.where(n < NB - 2, n + 1, jnp.where(n == NB - 2, 0, NB - 1))


class Links:
    def __init__(self):
        self.lat = lax.axis_index("lat")
        self.lon = lax.axis_index("lon")
        lat, lon = self.lat, self.lon
        self.top = lat == N_LAT - 1
        self.low = lat > 0
        self.inner = jnp.logical_not(self.top)
        self.left = lax.rem(lon + N_LON - 1, N_LON)
        self.right = lax.rem(lon + 1, N_LON)
        self.up = jnp.where(self.top, lat, lat + 1)
        self.down = jnp.where(self.low, lat - 1, lat)
        self.f0 = jnp.where(self.top, N_LON - 1 - lon, lon)
        self.fl = jnp.where(self.top, lax.rem(N_LON - lon, N_LON), self.left)
        self.fr = jnp.where(self.top, lax.rem(2 * N_LON - 2 - lon, N_LON), self.right)
        self.far_l = jnp.logical_not(self.top & (self.fl == lon))
        self.far_r = jnp.logical_not(self.top & (self.fr == lon))

    def greet(self):
        barrier = pltpu.get_barrier_semaphore()

        def signal(a, b):
            pl.semaphore_signal(barrier, inc=1, device_id=(a, b), device_id_type=MESH)

        def along_lon(d, _):
            signal(self.lat, lax.rem(self.lon + d, N_LON))
            return 0

        def along_lat(d, _):
            signal(lax.rem(self.lat + d, N_LAT), self.lon)
            return 0

        lax.fori_loop(1, N_LON, along_lon, 0)
        lax.fori_loop(1, N_LAT, along_lat, 0)

        @pl.when(self.inner)
        def _():
            signal(self.up, self.left)
            signal(self.up, self.right)

        @pl.when(self.low)
        def _():
            signal(self.down, self.left)
            signal(self.down, self.right)

    def met(self):
        count = N_LON + N_LAT - 2 + jnp.where(self.inner, 2, 0) + jnp.where(self.low, 2, 0)
        pl.semaphore_wait(pltpu.get_barrier_semaphore(), count)


def copy(src, dst, send, recv, a, b):
    return pltpu.make_async_remote_copy(src_ref=src, dst_ref=dst, send_sem=send, recv_sem=recv,
                                        device_id=(a, b), device_id_type=MESH)


def when(cond, todo):
    @pl.when(cond)
    def _():
        todo()


class ColumnExchange:
    def __init__(self, lk, lcols, rcols, hc, rows, send, recv, base):
        to_l, to_r = pl.ds(0, 16), pl.ds(16, 16)
        self.copies = []
        for k, (start, n) in enumerate(rows):
            own, dst = pl.ds(start, n), pl.ds(start + 3, n)
            s = base + 2 * k
            self.copies += [copy(rcols.at[own], hc.at[dst, to_l], send.at[s], recv.at[s], lk.lat, lk.right),
                            copy(lcols.at[own], hc.at[dst, to_r], send.at[s + 1], recv.at[s + 1], lk.lat, lk.left)]

    def start(self):
        for c in self.copies:
            c.start()

    def wait(self):
        for c in self.copies:
            c.wait()


class RowExchange:
    def __init__(self, lk, first, last, to_lo, to_hi, to_fold, lcols, rcols, hc, send, recv):
        self.lk = lk
        lo, hi = pl.ds(0, 3), pl.ds(ROWS + 3, 3)
        to_l, to_r = pl.ds(0, 16), pl.ds(16, 16)
        l_first, l_last = lcols.at[pl.ds(0, 3)], lcols.at[pl.ds(ROWS - 3, 3)]
        r_first, r_last = rcols.at[pl.ds(0, 3)], rcols.at[pl.ds(ROWS - 3, 3)]
        self.up_n = copy(last, to_lo, send.at[1], recv.at[0], lk.up, lk.f0)
        self.up_f = copy(last, to_fold, send.at[1], recv.at[1], lk.up, lk.f0)
        self.ul_n = copy(l_last, hc.at[lo, to_r], send.at[4], recv.at[3], lk.up, lk.fl)
        self.ul_f = copy(l_last, hc.at[hi, to_l], send.at[4], recv.at[4], lk.up, lk.fl)
        self.ur_n = copy(r_last, hc.at[lo, to_l], send.at[5], recv.at[2], lk.up, lk.fr)
        self.ur_f = copy(r_last, hc.at[hi, to_r], send.at[5], recv.at[5], lk.up, lk.fr)
        self.dn = copy(first, to_hi, send.at[0], recv.at[1], lk.down, lk.lon)
        self.dl = copy(l_first, hc.at[hi, to_r], send.at[2], recv.at[5], lk.down, lk.left)
        self.dr = copy(r_first, hc.at[hi, to_l], send.at[3], recv.at[4], lk.down, lk.right)
        self.own_l = pltpu.make_async_copy(l_last, hc.at[hi, to_l], send.at[4])
        self.own_r = pltpu.make_async_copy(r_last, hc.at[hi, to_r], send.at[5])

    def start(self):
        lk = self.lk

        def inner():
            self.ul_n.start()
            self.ur_n.start()
            self.up_n.start()

        def low():
            self.dl.start()
            self.dr.start()
            self.dn.start()

        when(lk.inner, inner)
        when(lk.top & lk.far_l, self.ul_f.start)
        when(lk.top & lk.far_r, self.ur_f.start)
        when(jnp.logical_not(lk.far_l), self.own_l.start)
        when(jnp.logical_not(lk.far_r), self.own_r.start)
        when(lk.top, self.up_f.start)
        when(lk.low, low)

    def wait(self):
        lk = self.lk

        def low():
            self.up_n.wait_recv()
            self.ul_n.wait_recv()
            self.ur_n.wait_recv()
            self.dn.wait_send()
            self.dl.wait_send()
            self.dr.wait_send()

        when(lk.inner, self.dn.wait_recv)
        when(lk.top, self.up_f.wait_recv)
        when(lk.far_l, self.dr.wait_recv)
        when(lk.far_r, self.dl.wait_recv)
        when(jnp.logical_not(lk.far_l), self.own_l.wait)
        when(jnp.logical_not(lk.far_r), self.own_r.wait)
        when(lk.low, low)
        self.up_n.wait_send()
        when(lk.far_l, self.ul_n.wait_send)
        when(lk.far_r, self.ur_n.wait_send)


def fan(make, n, wait):
    def go(d, _):
        if wait:
            make(d).wait()
        else:
            make(d).start()
        return 0

    lax.fori_loop(1, n, go, 0)


def kernel(x, mask, cot_hbm, taps1, bias, gain, w_in, w_out, scale,
           upd_hbm, out_hbm, o_in, o_out, o_k, o_bias, o_gain,
           cot, upd, out, ext, ext2, wmat, taps, perm, rim_a, rim_b, w_in_t, w_out_t,
           raw_s, rest_s, up_s, mask_s, last_s, edge, hr, hc, hr2, hc2, fold, gin, gout, gks, small,
           wb, c1, c2, c3, r1, r2, r3, q1, q2,
           io, cs, cr, rs, rr, cs2, cr2, rs2, rr2, a1, b1, a2, b2, a3, b3, a4, b4, a5, b5):
    lk = Links()
    lat, lon = lk.lat, lk.lon
    for cond, e0 in ((jnp.logical_not(lk.low), 0), (lk.top, ROWS + 3)):
        @pl.when(cond)
        def _():
            for e in range(3):
                ext2[e0 + e] = jnp.zeros((22, 16, C), bf16)

    lk.greet()
    cot_in = pltpu.make_async_copy(cot_hbm, cot, io.at[0])
    cot_in.start()

    lane = iota2((1, COLS), 1)
    h32 = iota2((1, 32), 1)
    perm[...] = one_hot(swap(iota2((COLS, 1), 0)) == lane)
    place = rim_place()
    rim_a[...] = one_hot(place == lane)
    rim_b[...] = one_hot(place == jnp.where(h32 < 16, h32 - 16, 240 + h32))

    for t in range(49):
        taps[t] = jnp.broadcast_to(taps1[t // 7, t % 7:t % 7 + 1], (16, C))
    eye = one_hot(iota2((C, 1), 0) == iota2((1, C), 1))
    zero = jnp.zeros((C, C), bf16)
    for j in range(4):
        for b in range(7):
            for i in range(2):
                for o in range(2):
                    a = 2 * j + i - o
                    blk = eye * taps1[a, b:b + 1] if 0 <= a < 7 else zero
                    r0 = (j * 7 + b) * 256 + i * C
                    wmat[r0:r0 + C, o * C:(o + 1) * C] = blk
    w_in_t[...] = w_in[...].T
    w_out_t[...] = w_out[...].T
    for ref in (gin, gout, small, gks):
        ref[...] = jnp.zeros_like(ref)

    def build(t, _):
        for j in (2 * t, 2 * t + 1):
            full = dot(perm[...], jnp.concatenate([x[2 * j], x[2 * j + 1]], axis=-1)).astype(bf16)
            ext[2 * j + 3, 3:19] = full[:, :C].reshape(16, 16, C)
            ext[2 * j + 4, 3:19] = full[:, C:].reshape(16, 16, C)
        return 0

    lax.fori_loop(0, ROWS // 4, build, 0)

    cols1 = ColumnExchange(lk, x.at[:, pl.ds(0, 16)], x.at[:, pl.ds(COLS - 16, 16)], hc, [(0, ROWS)], cs, cr, 0)
    rows1 = RowExchange(lk, x.at[pl.ds(0, 3)], x.at[pl.ds(ROWS - 3, 3)], hr.at[pl.ds(0, 3)], hr.at[pl.ds(3, 3)],
                        hr.at[pl.ds(3, 3)], x.at[:, pl.ds(0, 16)], x.at[:, pl.ds(COLS - 16, 16)], hc, rs, rr)
    lk.met()
    cols1.start()
    rows1.start()

    ones = jnp.ones((COLS, C), bf16)

    def mask_rows(t, _):
        for row in (2 * t, 2 * t + 1):
            pmask = perm[...] * mask[pl.ds(row, 1), :].astype(f32).astype(bf16)
            pair = dot(pmask, jnp.concatenate([cot[row], ones], axis=-1)).astype(bf16)
            up_s[row] = pair[:, :C]
            mask_s[row] = pair[:, C:]
        return 0

    cot_in.wait()
    lax.fori_loop(0, ROWS // 2, mask_rows, 0)

    def put_rim(dst, e, rim):
        rim = rim.astype(bf16).reshape(6, 16, C)
        dst[e, 0:3] = rim[0:3]
        dst[e, 19:22] = rim[3:6]

    def rims1(t, _):
        for j in (2 * t, 2 * t + 1):
            main = jnp.concatenate([x[2 * j], x[2 * j + 1]], axis=-1)
            side = jnp.concatenate([hc[2 * j + 3], hc[2 * j + 4]], axis=-1)
            rim = dot(rim_a[...], main) + dot(rim_b[...], side)
            put_rim(ext, 2 * j + 3, rim[:, :C])
            put_rim(ext, 2 * j + 4, rim[:, C:])
        return 0

    cols1.wait()
    lax.fori_loop(0, ROWS // 4, rims1, 0)

    def edges1():
        rows1.wait()
        zero_m = jnp.zeros((COLS, C), bf16)
        zero_s = jnp.zeros((32, C), bf16)
        for e in range(3):
            main = jnp.where(lk.low, hr[e], zero_m)
            side = jnp.where(lk.low, hc[e], zero_s)
            ext[e, 3:19] = dot(perm[...], main).astype(bf16).reshape(16, 16, C)
            put_rim(ext, e, dot(rim_a[...], main) + dot(rim_b[...], side))
        where = jnp.where(lk.top, 255 - lane, lane)
        own = one_hot(swap(iota2((COLS, 1), 0)) == where)
        ra = one_hot(place == where)
        side_col = jnp.where(lk.top, jnp.where(h32 < 16, -1 - h32, 287 - h32), jnp.where(h32 < 16, h32 - 16, 240 + h32))
        rb = one_hot(place == side_col)
        for m in range(3):
            src = jnp.where(lk.top, 2 - m, m)
            main = hr[3 + src]
            ext[35 + m, 3:19] = dot(own, main).astype(bf16).reshape(16, 16, C)
            put_rim(ext, 35 + m, dot(ra, main) + dot(rb, hc[35 + src]))

    cut = [(0, 16), (28, 4)]
    l_edge, r_edge = edge.at[:, pl.ds(0, 16)], edge.at[:, pl.ds(16, 16)]
    cols2a = ColumnExchange(lk, l_edge, r_edge, hc2, cut, cs2, cr2, 0)
    cols2b = ColumnExchange(lk, l_edge, r_edge, hc2, [(16, 12)], cs2, cr2, 4)
    rows2 = RowExchange(lk, ext2.at[pl.ds(3, 3), pl.ds(3, 16)], ext2.at[pl.ds(ROWS, 3), pl.ds(3, 16)],
                        ext2.at[pl.ds(0, 3), pl.ds(3, 16)], ext2.at[pl.ds(ROWS + 3, 3), pl.ds(3, 16)], hr2,
                        l_edge, r_edge, hc2, rs2, rr2)

    def sends2():
        cols2a.start()
        rows2.start()

    hs = iota2((32, 1), 0)
    sel = one_hot(jnp.where(hs < 16, hs, 224 + hs) == swap(lane))

    def conv_block(blk):
        part = conv_part(ext, blk * R, wmat, False, 0, 7)
        for r in range(R):
            for k0 in (0, 8):
                conv_rest(ext, taps, blk * R + r, r % 2, k0, rest_s.at[r])
        part = part + conv_part(ext, blk * R, wmat, False, 7, 14)
        raw_s[...] = part

    def mlp_pair(blk, p):
        units, invs, norms = [], [], []
        top = p * COLS if isinstance(p, int) else pl.multiple_of(p * COLS, COLS)
        for o in range(2):
            raw = raw_s[pl.ds(top, COLS), o * C:(o + 1) * C] + rest_s[2 * p + o] + bias[...]
            centre = jnp.mean(raw, axis=-1, keepdims=True)
            shifted = raw - centre
            var = jnp.mean(shifted * shifted, axis=-1, keepdims=True)
            inv = lax.rsqrt(var + epsilon)
            unit = shifted * inv
            units.append(unit)
            invs.append(inv)
            norms.append((unit * gain[...]).astype(bf16))
        norm = jnp.concatenate(norms, axis=0)
        first_row = blk * R + 2 * p
        up = jnp.concatenate([up_s[first_row], up_s[first_row + 1]], axis=0)
        mixed, bn = None, None
        halves = range(0, HID, 256)
        ready = [(dot(norm, w_in[:, f:f + 256]).astype(bf16), dot(up, w_out_t[:, f:f + 256]).astype(bf16)) for f in halves]
        for f, (pre, bh) in zip(halves, ready):
            hid, der = gelu_parts(pre)
            bp = bh * der
            mx = dot(hid, w_out[f:f + 256])
            bx = dot(bp, w_in_t[f:f + 256])
            mixed = mx if mixed is None else mixed + mx
            bn = bx if bn is None else bn + bx
            gin[:, f:f + 256] += dot_t(norm, bp)
            gout[:, f:f + 256] += dot_t(up, hid)
        mixed = mixed.astype(bf16)
        bcs = []
        for o in range(2):
            half = slice(o * COLS, (o + 1) * COLS)
            unit = units[o]
            bnf = bn[half].astype(bf16).astype(f32)
            g = bnf * gain[...]
            m1 = jnp.mean(g, axis=-1, keepdims=True)
            m2 = jnp.mean(g * unit, axis=-1, keepdims=True)
            bc = ((g - m1 - unit * m2) * invs[o]).astype(bf16)
            small[0:8] += jnp.sum((bnf * unit).reshape(COLS // 8, 8, C), axis=0)
            small[8:16] += jnp.sum(bc.astype(f32).reshape(COLS // 8, 8, C), axis=0)
            ext2[first_row + o + 3, 3:19] = bc.reshape(16, 16, C)
            bcs.append(bc)
        nat = dot(perm[...], jnp.concatenate([mixed[o * COLS:(o + 1) * COLS] * mask_s[first_row + o] for o in range(2)], axis=-1))
        ends = dot(sel, jnp.concatenate(bcs, axis=-1)).astype(bf16)
        for o in range(2):
            row = first_row + o
            upd[row] = (x[row].astype(f32) + nat[:, o * C:(o + 1) * C]).astype(bf16)
            edge[row] = ends[:, o * C:(o + 1) * C]

    def main_step(n, _):
        when(n == FIRST, edges1)
        when(n == FIRST + 2, sends2)
        blk = main_block(n)
        conv_block(blk)

        @pl.when(n < NB)
        def _():
            for p in range(2):
                mlp_pair(blk, p)
        return 0

    lax.fori_loop(0, NB, main_step, 0)

    upd_out = pltpu.make_async_copy(upd, upd_hbm, io.at[1])
    upd_out.start()
    cols2b.start()

    def hop1(d):
        to = lax.rem(lon + d, N_LON)
        return copy(wb.at[to], r1.at[d], a1.at[d], b1.at[d], lat, to)

    def hop2(d):
        return copy(c1, r2.at[lat], a2.at[d], b2.at[d], lax.rem(lat + d, N_LAT), lon)

    def hop3(d):
        return copy(c2, r3.at[lon], a3.at[d], b3.at[d], lat, lax.rem(lon + d, N_LON))

    def hop4(d):
        return copy(c3, q1.at[lon], a4.at[d], b4.at[d], lat, lax.rem(lon + d, N_LON))

    def hop5(d):
        return copy(c3, q2.at[lat], a5.at[d], b5.at[d], lax.rem(lat + d, N_LAT), lon)

    for c in range(N_LON):
        r0, c0 = c // 4 * 32, c % 4 * C
        wb[c, 0:32] = gin[r0:r0 + 32, c0:c0 + C].astype(bf16)
        wb[c, 32:SEG] = gout[r0:r0 + 32, c0:c0 + C].astype(bf16)
    fan(hop1, N_LON, False)

    def w_second():
        fan(hop1, N_LON, True)
        total = wb[lon].astype(f32)
        for d in range(1, N_LON):
            total = total + r1[d].astype(f32)
        c1[...] = total.astype(bf16)
        r2[lat] = c1[...]
        fan(hop2, N_LAT, False)

    def w_third():
        fan(hop2, N_LAT, True)
        total = r2[0].astype(f32)
        for d in range(1, N_LAT):
            total = total + r2[d].astype(f32)
        c2[...] = (total * scale[0]).astype(bf16)
        r3[lon] = c2[...]
        fan(hop3, N_LON, False)

    def rim2(e, row):
        main = ext2[e, 3:19].reshape(COLS, C)
        ra = one_hot(place == swap(lane))
        put_rim(ext2, e, dot(ra, main) + dot(rim_b[...], hc2[e]))

    def rims2(t, _):
        ra = one_hot(place == swap(lane))
        for j in (2 * t, 2 * t + 1):
            main = jnp.concatenate([ext2[2 * j + 3, 3:19].reshape(COLS, C), ext2[2 * j + 4, 3:19].reshape(COLS, C)], axis=-1)
            side = jnp.concatenate([hc2[2 * j + 3], hc2[2 * j + 4]], axis=-1)
            rim = dot(ra, main) + dot(rim_b[...], side)
            put_rim(ext2, 2 * j + 3, rim[:, :C])
            put_rim(ext2, 2 * j + 4, rim[:, C:])
        return 0

    cols2a.wait()
    lax.fori_loop(0, 4, rims2, 0)
    rims2(7, 0)

    def late_cols():
        cols2b.wait()
        lax.fori_loop(4, 7, rims2, 0)

    def edges2():
        rows2.wait()
        ra = one_hot(place == swap(lane))

        def rim(e):
            put_rim(ext2, e, dot(ra, ext2[e, 3:19].reshape(COLS, C)) + dot(rim_b[...], hc2[e]))

        def low():
            for e in range(3):
                rim(e)

        def inner():
            for e in range(3):
                rim(35 + e)

        def top():
            own = one_hot(swap(iota2((COLS, 1), 0)) == 255 - swap(lane))
            fa = one_hot(place == 255 - swap(lane))
            fb = one_hot(place == jnp.where(h32 < 16, -1 - h32, 287 - h32))
            for m in range(3):
                main = hr2[2 - m].reshape(COLS, C)
                fold[m, 3:19] = dot(own, main).astype(bf16).reshape(16, 16, C)
                put_rim(fold, m, dot(fa, main) + dot(fb, hc2[37 - m]))

        when(lk.low, low)
        when(lk.inner, inner)
        when(lk.top, top)

    def tap_sums(src, e, row, a, flip):
        for b in range(7):
            total = None
            for k0 in (0, 8):
                q = src[e, k0 + b] * ext[row + 3, 3 + k0]
                for k in range(k0 + 1, k0 + 8):
                    q = q + src[e, k + b] * ext[row + 3, 3 + k]
                total = q if total is None else total + q
            q = total.astype(f32)
            t = a * 7 + b
            gks[(48 - t) if flip else t] += q[:8] + q[8:]

    def finish(t, _):
        nat = dot(perm[...], last_s[t])
        for o in range(2):
            out[2 * t + o] = (cot[2 * t + o].astype(f32) + nat[:, (1 - o) * C:(2 - o) * C]).astype(bf16)
        return 0

    def back_step(n, _):
        when(n == 2, late_cols)
        when(n == 3, w_second)
        when(n == 5, w_third)
        when(n == NB - 2, edges2)
        row = back_block(n) * R
        conv = None
        for j in range(3):
            part = conv_part(ext2, row, wmat, True, 7 * j, 7 * j + 7)
            conv = part if conv is None else conv + part
            for t in range(28 * j // 3, 28 * (j + 1) // 3):
                tap_sums(ext2, row + t // 7 + t % 7, row + t // 7, t % 7, True)
        for p in range(2):
            rest = jnp.concatenate([conv_first(ext2, taps, row + 2 * p, o) for o in (1, 0)], axis=-1)
            last_s[back_block(n) * 2 + p] = (conv[p * COLS:(p + 1) * COLS] + rest).astype(bf16)
        return 0

    lax.fori_loop(0, NB, back_step, 0)
    @pl.when(lk.top)
    def _():
        for t in range(3):
            for m in range(t + 1):
                tap_sums(fold, m, ROWS - 3 + t, 6 - t + m, False)

    rest = [jnp.sum(gks[t], axis=0, keepdims=True) for t in range(49)]
    rest += [jnp.sum(small[:8], axis=0, keepdims=True), jnp.sum(small[8:], axis=0, keepdims=True), jnp.zeros((13, C), f32)]
    c3[...] = jnp.concatenate(rest, axis=0).astype(bf16)
    fan(hop4, N_LON, False)
    q1[lon] = c3[...]

    def fold_conv():
        for t in range(3):
            acc = [None] * 16
            for m in range(t + 1):
                a = 6 - t + m
                for k in range(16):
                    p = fold[m, k] * taps[a * 7]
                    for b in range(1, 7):
                        p = p + fold[m, k + b] * taps[a * 7 + b]
                    p = p.astype(f32)
                    acc[k] = p if acc[k] is None else acc[k] + p
            row = ROWS - 3 + t
            side = slice((1 - row % 2) * C, (2 - row % 2) * C)
            last_s[row // 2, :, side] = (last_s[row // 2, :, side].astype(f32) + jnp.concatenate(acc, axis=0)).astype(bf16)

    when(lk.top, fold_conv)
    lax.fori_loop(0, ROWS // 2, finish, 0)
    out_out = pltpu.make_async_copy(out, out_hbm, io.at[0])
    out_out.start()
    fan(hop3, N_LON, True)
    for j in range(4):
        for k in range(4):
            o_in[32 * k:32 * k + 32, j * C:(j + 1) * C] = r3[4 * k + j, 0:32].astype(f32)
        whole = jnp.concatenate([r3[4 * k + j, 32:SEG] for k in range(4)], axis=0).astype(f32)
        o_out[j * C:(j + 1) * C] = whole.T
    fan(hop4, N_LON, True)
    total = q1[0].astype(f32)
    for d in range(1, N_LON):
        total = total + q1[d].astype(f32)
    c3[...] = total.astype(bf16)
    fan(hop5, N_LAT, False)
    q2[lat] = c3[...]
    fan(hop5, N_LAT, True)
    total = q2[0].astype(f32)
    for d in range(1, N_LAT):
        total = total + q2[d].astype(f32)
    total = total * scale[0]
    for a in range(7):
        o_k[a] = total[7 * a:7 * a + 7]
    o_gain[...] = total[49:50]
    o_bias[...] = total[50:51]
    upd_out.wait()
    out_out.wait()


def hand_over(*refs):
    for a, b in zip(refs[:5], refs[5:]):
        b[...] = a[...]


def body(ocean_state, sea_mask, depth_kernel, conv_bias, norm_gain, w_in, w_out, cotangent):
    cells = COLS * ROWS * lax.axis_size("lat") * lax.axis_size("lon")
    scale = 1.0 / jnp.sqrt(jnp.full((1,), cells, f32))
    vm = pl.BlockSpec(memory_space=pltpu.VMEM)
    hbm = pl.BlockSpec(memory_space=pl.ANY)
    dma = pltpu.SemaphoreType.DMA
    V = pltpu.VMEM
    tile = jax.ShapeDtypeStruct((ROWS, COLS, C), bf16)
    upd, grad_state, o_in, o_out, o_k, o_bias, o_gain = pl.pallas_call(
        kernel,
        in_specs=[vm, vm, hbm, vm, vm, vm, vm, vm, pl.BlockSpec(memory_space=pltpu.SMEM)],
        out_specs=[hbm, hbm] + [vm] * 5,
        out_shape=[tile, tile, jax.ShapeDtypeStruct((C, HID), f32), jax.ShapeDtypeStruct((HID, C), f32),
                   jax.ShapeDtypeStruct((7, 7, C), f32), jax.ShapeDtypeStruct((1, C), f32), jax.ShapeDtypeStruct((1, C), f32)],
        scratch_shapes=[
            V((ROWS, COLS, C), bf16), V((ROWS, COLS, C), bf16), V((ROWS, COLS, C), bf16),
            V((38, 22, 16, C), bf16), V((38, 22, 16, C), bf16), V((28 * 256, 256), bf16), V((49, 16, C), bf16),
            V((COLS, COLS), bf16), V((96, COLS), bf16), V((96, 32), bf16), V((HID, C), bf16), V((C, HID), bf16),
            V((2 * COLS, 2 * C), f32), V((R, COLS, C), f32), V((ROWS, COLS, C), bf16), V((ROWS, COLS, C), bf16), V((ROWS // 2, COLS, 2 * C), bf16),
            V((ROWS, 32, C), bf16), V((6, COLS, C), bf16), V((ROWS + 6, 32, C), bf16),
            V((3, 16, 16, C), bf16), V((ROWS + 6, 32, C), bf16), V((3, 22, 16, C), bf16),
            V((C, HID), f32), V((C, HID), f32), V((49, 8, C), f32), V((16, C), f32),
            V((N_LON, SEG, C), bf16), V((SEG, C), bf16), V((SEG, C), bf16), V((SEG, C), bf16),
            V((N_LON, SEG, C), bf16), V((N_LAT, SEG, C), bf16), V((N_LON, SEG, C), bf16),
            V((N_LON, SEG, C), bf16), V((N_LAT, SEG, C), bf16),
            dma((2,)), dma((2,)), dma((2,)), dma((6,)), dma((6,)), dma((6,)), dma((6,)), dma((6,)), dma((6,)),
            dma((N_LON,)), dma((N_LON,)), dma((N_LAT,)), dma((N_LAT,)), dma((N_LON,)), dma((N_LON,)),
            dma((N_LON,)), dma((N_LON,)), dma((N_LAT,)), dma((N_LAT,))],
        compiler_params=pltpu.CompilerParams(collective_id=0, has_side_effects=True, vmem_limit_bytes=VLIM),
        name="block_step",
    )(ocean_state, sea_mask, cotangent, depth_kernel, conv_bias.reshape(1, C), norm_gain.reshape(1, C), w_in, w_out, scale)
    smalls = (o_k, o_bias, o_gain, o_in, o_out)
    o_k, o_bias, o_gain, o_in, o_out = pl.pallas_call(
        hand_over,
        in_specs=[vm] * 5,
        out_specs=[vm] * 5,
        out_shape=[jax.ShapeDtypeStruct(a.shape, a.dtype) for a in smalls],
        name="hand_over",
    )(*smalls)
    return upd, grad_state, o_k, o_bias.reshape(C), o_gain.reshape(C), o_in, o_out


def solution(mesh):
    tile = P("lat", "lon", None)
    return jax.shard_map(
        body,
        mesh=mesh,
        in_specs=(tile, P("lat", "lon"), P(), P(), P(), P(), P(), tile),
        out_specs=(tile, tile, P(), P(), P(), P(), P()),
        check_vma=False,
    )
```

```python
import functools
import jax
import jax.numpy as jnp
from jax import lax
from jax.experimental import pallas as pl
from jax.experimental.pallas import tpu as pltpu
from jax.sharding import PartitionSpec as P

MESH = pl.DeviceIdType.MESH
bf16 = jnp.bfloat16
f32 = jnp.float32
epsilon = 1e-06
root_half = 0.7978845608028654
cubic_coef = 0.044715
z_one = -2.0 * root_half * 1.4426950408889634
z_three = -2.0 * root_half * cubic_coef * 1.4426950408889634

C = 128
ROWS = 32
COLS = 256
HID = 512
EXT = 22 * 16
N_LON = 16
N_LAT = 8
SEG = 64
R = 4
NB = ROWS // R
FIRST = 3
MX_TAPS = 14
VLIM = 60 * 1024 * 1024


def iota2(shape, dim):
    return lax.broadcasted_iota(jnp.int32, shape, dim)


def one_hot(hit):
    return jnp.where(hit, 1.0, 0.0).astype(bf16)


def swap(o):
    return (o % 16) * 16 + o // 16


def rim_place():
    o = iota2((96, 1), 0)
    o = jnp.where(o >= 48, o + 256, o)
    return (o % 16) * 16 + o // 16 - 3


def dot(a, b):
    return jnp.dot(a, b, preferred_element_type=f32)


def dot_t(a, b):
    return lax.dot_general(a, b, (((0,), (0,)), ((), ())), preferred_element_type=f32)


def conv_part(ext, row, wmat, flip, lo, hi):
    sides = []
    for pair_row in (row, row + 2):
        parts = []
        for u in range(lo, hi):
            j, b = u // 7, u % 7
            e = pair_row + 2 * (3 - j if flip else j)
            s = 6 - b if flip else b
            pair = [ext[e, s:s + 16].reshape(COLS, C), ext[e + 1, s:s + 16].reshape(COLS, C)]
            parts += pair[::-1] if flip else pair
        sides.append(jnp.concatenate(parts, axis=-1))
    return dot(jnp.concatenate(sides, axis=0), wmat[lo * 256:hi * 256])


def conv_rest(ext, taps, row, o, k0, dst):
    acc = [None] * 8
    for a in range(MX_TAPS // 7 * 2 - o, 7):
        win = [ext[row + a, k0 + k] for k in range(14)]
        w = [taps[a * 7 + b] for b in range(7)]
        for k in range(8):
            p = win[k] * w[0]
            for b in range(1, 7):
                p = p + win[k + b] * w[b]
            p = p.astype(f32)
            acc[k] = p if acc[k] is None else acc[k] + p
    for k in range(8):
        dst[(k0 + k) * 16:(k0 + k + 1) * 16] = acc[k]


def conv_first(ext, taps, row, o):
    acc = [None] * 16
    for a in range(2 - o):
        w = [taps[48 - a * 7 - b] for b in range(7)]
        for k in range(16):
            p = ext[row + o + a, k] * w[0]
            for b in range(1, 7):
                p = p + ext[row + o + a, k + b] * w[b]
            p = p.astype(f32)
            acc[k] = p if acc[k] is None else acc[k] + p
    return jnp.concatenate(acc, axis=0)


def gelu_parts(v):
    u = v * v
    z = jnp.minimum(v * (z_one + z_three * u), 80.0)
    e = jnp.exp2(z)
    h = pl.reciprocal(e + 1.0, approx=True)
    act = v * h
    der = h + (act * (e * h)) * (2.0 * root_half + (6.0 * root_half * cubic_coef) * u)
    return act, der


def main_block(n):
    return jnp.where(n < FIRST, n + 1, jnp.where(n == FIRST, 0, jnp.where(n == FIRST + 1, NB - 1, n - 1)))


def back_block(n):
    return jnp.where(n < NB - 2, n + 1, jnp.where(n == NB - 2, 0, NB - 1))


class Links:
    def __init__(self):
        self.lat = lax.axis_index("lat")
        self.lon = lax.axis_index("lon")
        lat, lon = self.lat, self.lon
        self.top = lat == N_LAT - 1
        self.low = lat > 0
        self.inner = jnp.logical_not(self.top)
        self.left = lax.rem(lon + N_LON - 1, N_LON)
        self.right = lax.rem(lon + 1, N_LON)
        self.up = jnp.where(self.top, lat, lat + 1)
        self.down = jnp.where(self.low, lat - 1, lat)
        self.f0 = jnp.where(self.top, N_LON - 1 - lon, lon)
        self.fl = jnp.where(self.top, lax.rem(N_LON - lon, N_LON), self.left)
        self.fr = jnp.where(self.top, lax.rem(2 * N_LON - 2 - lon, N_LON), self.right)
        self.far_l = jnp.logical_not(self.top & (self.fl == lon))
        self.far_r = jnp.logical_not(self.top & (self.fr == lon))

    def greet(self):
        barrier = pltpu.get_barrier_semaphore()

        def signal(a, b):
            pl.semaphore_signal(barrier, inc=1, device_id=(a, b), device_id_type=MESH)

        def along_lon(d, _):
            signal(self.lat, lax.rem(self.lon + d, N_LON))
            return 0

        def along_lat(d, _):
            signal(lax.rem(self.lat + d, N_LAT), self.lon)
            return 0

        lax.fori_loop(1, N_LON, along_lon, 0)
        lax.fori_loop(1, N_LAT, along_lat, 0)

        @pl.when(self.inner)
        def _():
            signal(self.up, self.left)
            signal(self.up, self.right)

        @pl.when(self.low)
        def _():
            signal(self.down, self.left)
            signal(self.down, self.right)

    def met(self):
        count = N_LON + N_LAT - 2 + jnp.where(self.inner, 2, 0) + jnp.where(self.low, 2, 0)
        pl.semaphore_wait(pltpu.get_barrier_semaphore(), count)


def copy(src, dst, send, recv, a, b):
    return pltpu.make_async_remote_copy(src_ref=src, dst_ref=dst, send_sem=send, recv_sem=recv,
                                        device_id=(a, b), device_id_type=MESH)


def when(cond, todo):
    @pl.when(cond)
    def _():
        todo()


class ColumnExchange:
    def __init__(self, lk, lcols, rcols, hc, rows, send, recv, base):
        to_l, to_r = pl.ds(0, 16), pl.ds(16, 16)
        self.copies = []
        for k, (start, n) in enumerate(rows):
            own, dst = pl.ds(start, n), pl.ds(start + 3, n)
            s = base + 2 * k
            self.copies += [copy(rcols.at[own], hc.at[dst, to_l], send.at[s], recv.at[s], lk.lat, lk.right),
                            copy(lcols.at[own], hc.at[dst, to_r], send.at[s + 1], recv.at[s + 1], lk.lat, lk.left)]

    def start(self):
        for c in self.copies:
            c.start()

    def wait(self):
        for c in self.copies:
            c.wait()


class RowExchange:
    def __init__(self, lk, first, last, to_lo, to_hi, to_fold, lcols, rcols, hc, send, recv):
        self.lk = lk
        lo, hi = pl.ds(0, 3), pl.ds(ROWS + 3, 3)
        to_l, to_r = pl.ds(0, 16), pl.ds(16, 16)
        l_first, l_last = lcols.at[pl.ds(0, 3)], lcols.at[pl.ds(ROWS - 3, 3)]
        r_first, r_last = rcols.at[pl.ds(0, 3)], rcols.at[pl.ds(ROWS - 3, 3)]
        self.up_n = copy(last, to_lo, send.at[1], recv.at[0], lk.up, lk.f0)
        self.up_f = copy(last, to_fold, send.at[1], recv.at[1], lk.up, lk.f0)
        self.ul_n = copy(l_last, hc.at[lo, to_r], send.at[4], recv.at[3], lk.up, lk.fl)
        self.ul_f = copy(l_last, hc.at[hi, to_l], send.at[4], recv.at[4], lk.up, lk.fl)
        self.ur_n = copy(r_last, hc.at[lo, to_l], send.at[5], recv.at[2], lk.up, lk.fr)
        self.ur_f = copy(r_last, hc.at[hi, to_r], send.at[5], recv.at[5], lk.up, lk.fr)
        self.dn = copy(first, to_hi, send.at[0], recv.at[1], lk.down, lk.lon)
        self.dl = copy(l_first, hc.at[hi, to_r], send.at[2], recv.at[5], lk.down, lk.left)
        self.dr = copy(r_first, hc.at[hi, to_l], send.at[3], recv.at[4], lk.down, lk.right)
        self.own_l = pltpu.make_async_copy(l_last, hc.at[hi, to_l], send.at[4])
        self.own_r = pltpu.make_async_copy(r_last, hc.at[hi, to_r], send.at[5])

    def start(self):
        lk = self.lk

        def inner():
            self.ul_n.start()
            self.ur_n.start()
            self.up_n.start()

        def low():
            self.dl.start()
            self.dr.start()
            self.dn.start()

        when(lk.inner, inner)
        when(lk.top & lk.far_l, self.ul_f.start)
        when(lk.top & lk.far_r, self.ur_f.start)
        when(jnp.logical_not(lk.far_l), self.own_l.start)
        when(jnp.logical_not(lk.far_r), self.own_r.start)
        when(lk.top, self.up_f.start)
        when(lk.low, low)

    def wait(self):
        lk = self.lk

        def low():
            self.up_n.wait_recv()
            self.ul_n.wait_recv()
            self.ur_n.wait_recv()
            self.dn.wait_send()
            self.dl.wait_send()
            self.dr.wait_send()

        when(lk.inner, self.dn.wait_recv)
        when(lk.top, self.up_f.wait_recv)
        when(lk.far_l, self.dr.wait_recv)
        when(lk.far_r, self.dl.wait_recv)
        when(jnp.logical_not(lk.far_l), self.own_l.wait)
        when(jnp.logical_not(lk.far_r), self.own_r.wait)
        when(lk.low, low)
        self.up_n.wait_send()
        when(lk.far_l, self.ul_n.wait_send)
        when(lk.far_r, self.ur_n.wait_send)


def fan(make, n, wait):
    def go(d, _):
        if wait:
            make(d).wait()
        else:
            make(d).start()
        return 0

    lax.fori_loop(1, n, go, 0)


def kernel(x, mask, cot_hbm, taps1, bias, gain, w_in, w_out, scale,
           upd_hbm, out_hbm, o_in, o_out, o_k, o_bias, o_gain,
           cot, upd, out, ext, ext2, wmat, taps, perm, rim_a, rim_b, w_in_t, w_out_t,
           raw_s, rest_s, up_s, mask_s, last_s, edge, hr, hc, hr2, hc2, fold, gin, gout, gks, small,
           wb, c1, c2, c3, r1, r2, r3, q1, q2,
           io, cs, cr, rs, rr, cs2, cr2, rs2, rr2, a1, b1, a2, b2, a3, b3, a4, b4, a5, b5):
    lk = Links()
    lat, lon = lk.lat, lk.lon
    for cond, e0 in ((jnp.logical_not(lk.low), 0), (lk.top, ROWS + 3)):
        @pl.when(cond)
        def _():
            for e in range(3):
                ext2[e0 + e] = jnp.zeros((22, 16, C), bf16)

    lk.greet()
    cot_in = pltpu.make_async_copy(cot_hbm, cot, io.at[0])
    cot_in.start()

    lane = iota2((1, COLS), 1)
    h32 = iota2((1, 32), 1)
    perm[...] = one_hot(swap(iota2((COLS, 1), 0)) == lane)
    place = rim_place()
    rim_a[...] = one_hot(place == lane)
    rim_b[...] = one_hot(place == jnp.where(h32 < 16, h32 - 16, 240 + h32))

    for t in range(49):
        taps[t] = jnp.broadcast_to(taps1[t // 7, t % 7:t % 7 + 1], (16, C))
    eye = one_hot(iota2((C, 1), 0) == iota2((1, C), 1))
    zero = jnp.zeros((C, C), bf16)
    for j in range(4):
        for b in range(7):
            for i in range(2):
                for o in range(2):
                    a = 2 * j + i - o
                    blk = eye * taps1[a, b:b + 1] if 0 <= a < 7 else zero
                    r0 = (j * 7 + b) * 256 + i * C
                    wmat[r0:r0 + C, o * C:(o + 1) * C] = blk
    w_in_t[...] = w_in[...].T
    w_out_t[...] = w_out[...].T
    for ref in (gin, gout, small, gks):
        ref[...] = jnp.zeros_like(ref)

    def build(t, _):
        for j in (2 * t, 2 * t + 1):
            full = dot(perm[...], jnp.concatenate([x[2 * j], x[2 * j + 1]], axis=-1)).astype(bf16)
            ext[2 * j + 3, 3:19] = full[:, :C].reshape(16, 16, C)
            ext[2 * j + 4, 3:19] = full[:, C:].reshape(16, 16, C)
        return 0

    lax.fori_loop(0, ROWS // 4, build, 0)

    cols1 = ColumnExchange(lk, x.at[:, pl.ds(0, 16)], x.at[:, pl.ds(COLS - 16, 16)], hc, [(0, ROWS)], cs, cr, 0)
    rows1 = RowExchange(lk, x.at[pl.ds(0, 3)], x.at[pl.ds(ROWS - 3, 3)], hr.at[pl.ds(0, 3)], hr.at[pl.ds(3, 3)],
                        hr.at[pl.ds(3, 3)], x.at[:, pl.ds(0, 16)], x.at[:, pl.ds(COLS - 16, 16)], hc, rs, rr)
    lk.met()
    cols1.start()
    rows1.start()

    ones = jnp.ones((COLS, C), bf16)

    def mask_rows(t, _):
        for row in (2 * t, 2 * t + 1):
            pmask = perm[...] * mask[pl.ds(row, 1), :].astype(f32).astype(bf16)
            pair = dot(pmask, jnp.concatenate([cot[row], ones], axis=-1)).astype(bf16)
            up_s[row] = pair[:, :C]
            mask_s[row] = pair[:, C:]
        return 0

    cot_in.wait()
    lax.fori_loop(0, ROWS // 2, mask_rows, 0)

    def put_rim(dst, e, rim):
        rim = rim.astype(bf16).reshape(6, 16, C)
        dst[e, 0:3] = rim[0:3]
        dst[e, 19:22] = rim[3:6]

    def rims1(t, _):
        for j in (2 * t, 2 * t + 1):
            main = jnp.concatenate([x[2 * j], x[2 * j + 1]], axis=-1)
            side = jnp.concatenate([hc[2 * j + 3], hc[2 * j + 4]], axis=-1)
            rim = dot(rim_a[...], main) + dot(rim_b[...], side)
            put_rim(ext, 2 * j + 3, rim[:, :C])
            put_rim(ext, 2 * j + 4, rim[:, C:])
        return 0

    cols1.wait()
    lax.fori_loop(0, ROWS // 4, rims1, 0)

    def edges1():
        rows1.wait()
        zero_m = jnp.zeros((COLS, C), bf16)
        zero_s = jnp.zeros((32, C), bf16)
        for e in range(3):
            main = jnp.where(lk.low, hr[e], zero_m)
            side = jnp.where(lk.low, hc[e], zero_s)
            ext[e, 3:19] = dot(perm[...], main).astype(bf16).reshape(16, 16, C)
            put_rim(ext, e, dot(rim_a[...], main) + dot(rim_b[...], side))
        where = jnp.where(lk.top, 255 - lane, lane)
        own = one_hot(swap(iota2((COLS, 1), 0)) == where)
        ra = one_hot(place == where)
        side_col = jnp.where(lk.top, jnp.where(h32 < 16, -1 - h32, 287 - h32), jnp.where(h32 < 16, h32 - 16, 240 + h32))
        rb = one_hot(place == side_col)
        for m in range(3):
            src = jnp.where(lk.top, 2 - m, m)
            main = hr[3 + src]
            ext[35 + m, 3:19] = dot(own, main).astype(bf16).reshape(16, 16, C)
            put_rim(ext, 35 + m, dot(ra, main) + dot(rb, hc[35 + src]))

    cut = [(0, 16), (28, 4)]
    l_edge, r_edge = edge.at[:, pl.ds(0, 16)], edge.at[:, pl.ds(16, 16)]
    cols2a = ColumnExchange(lk, l_edge, r_edge, hc2, cut, cs2, cr2, 0)
    cols2b = ColumnExchange(lk, l_edge, r_edge, hc2, [(16, 12)], cs2, cr2, 4)
    rows2 = RowExchange(lk, ext2.at[pl.ds(3, 3), pl.ds(3, 16)], ext2.at[pl.ds(ROWS, 3), pl.ds(3, 16)],
                        ext2.at[pl.ds(0, 3), pl.ds(3, 16)], ext2.at[pl.ds(ROWS + 3, 3), pl.ds(3, 16)], hr2,
                        l_edge, r_edge, hc2, rs2, rr2)

    def sends2():
        cols2a.start()
        rows2.start()

    hs = iota2((32, 1), 0)
    sel = one_hot(jnp.where(hs < 16, hs, 224 + hs) == swap(lane))

    def conv_block(blk):
        part = conv_part(ext, blk * R, wmat, False, 0, 7)
        for r in range(R):
            for k0 in (0, 8):
                conv_rest(ext, taps, blk * R + r, r % 2, k0, rest_s.at[r])
        part = part + conv_part(ext, blk * R, wmat, False, 7, 14)
        raw_s[...] = part

    def mlp_pair(blk, p):
        units, invs, norms = [], [], []
        top = p * COLS if isinstance(p, int) else pl.multiple_of(p * COLS, COLS)
        for o in range(2):
            raw = raw_s[pl.ds(top, COLS), o * C:(o + 1) * C] + rest_s[2 * p + o] + bias[...]
            centre = jnp.mean(raw, axis=-1, keepdims=True)
            shifted = raw - centre
            var = jnp.mean(shifted * shifted, axis=-1, keepdims=True)
            inv = lax.rsqrt(var + epsilon)
            unit = shifted * inv
            units.append(unit)
            invs.append(inv)
            norms.append((unit * gain[...]).astype(bf16))
        norm = jnp.concatenate(norms, axis=0)
        first_row = blk * R + 2 * p
        up = jnp.concatenate([up_s[first_row], up_s[first_row + 1]], axis=0)
        mixed, bn = None, None
        halves = range(0, HID, 256)
        ready = [(dot(norm, w_in[:, f:f + 256]).astype(bf16), dot(up, w_out_t[:, f:f + 256]).astype(bf16)) for f in halves]
        for f, (pre, bh) in zip(halves, ready):
            hid, der = gelu_parts(pre)
            bp = bh * der
            mx = dot(hid, w_out[f:f + 256])
            bx = dot(bp, w_in_t[f:f + 256])
            mixed = mx if mixed is None else mixed + mx
            bn = bx if bn is None else bn + bx
            gin[:, f:f + 256] += dot_t(norm, bp)
            gout[:, f:f + 256] += dot_t(up, hid)
        mixed = mixed.astype(bf16)
        bcs = []
        for o in range(2):
            half = slice(o * COLS, (o + 1) * COLS)
            unit = units[o]
            bnf = bn[half].astype(bf16).astype(f32)
            g = bnf * gain[...]
            m1 = jnp.mean(g, axis=-1, keepdims=True)
            m2 = jnp.mean(g * unit, axis=-1, keepdims=True)
            bc = ((g - m1 - unit * m2) * invs[o]).astype(bf16)
            small[0:8] += jnp.sum((bnf * unit).reshape(COLS // 8, 8, C), axis=0)
            small[8:16] += jnp.sum(bc.astype(f32).reshape(COLS // 8, 8, C), axis=0)
            ext2[first_row + o + 3, 3:19] = bc.reshape(16, 16, C)
            bcs.append(bc)
        nat = dot(perm[...], jnp.concatenate([mixed[o * COLS:(o + 1) * COLS] * mask_s[first_row + o] for o in range(2)], axis=-1))
        ends = dot(sel, jnp.concatenate(bcs, axis=-1)).astype(bf16)
        for o in range(2):
            row = first_row + o
            upd[row] = (x[row].astype(f32) + nat[:, o * C:(o + 1) * C]).astype(bf16)
            edge[row] = ends[:, o * C:(o + 1) * C]

    def main_step(n, _):
        when(n == FIRST, edges1)
        when(n == FIRST + 2, sends2)
        blk = main_block(n)
        conv_block(blk)

        @pl.when(n < NB)
        def _():
            for p in range(2):
                mlp_pair(blk, p)
        return 0

    lax.fori_loop(0, NB, main_step, 0)

    upd_out = pltpu.make_async_copy(upd, upd_hbm, io.at[1])
    upd_out.start()
    cols2b.start()

    def hop1(d):
        to = lax.rem(lon + d, N_LON)
        return copy(wb.at[to], r1.at[d], a1.at[d], b1.at[d], lat, to)

    def hop2(d):
        return copy(c1, r2.at[lat], a2.at[d], b2.at[d], lax.rem(lat + d, N_LAT), lon)

    def hop3(d):
        return copy(c2, r3.at[lon], a3.at[d], b3.at[d], lat, lax.rem(lon + d, N_LON))

    def hop4(d):
        return copy(c3, q1.at[lon], a4.at[d], b4.at[d], lat, lax.rem(lon + d, N_LON))

    def hop5(d):
        return copy(c3, q2.at[lat], a5.at[d], b5.at[d], lax.rem(lat + d, N_LAT), lon)

    for c in range(N_LON):
        r0, c0 = c // 4 * 32, c % 4 * C
        wb[c, 0:32] = gin[r0:r0 + 32, c0:c0 + C].astype(bf16)
        wb[c, 32:SEG] = gout[r0:r0 + 32, c0:c0 + C].astype(bf16)
    fan(hop1, N_LON, False)

    def w_second():
        fan(hop1, N_LON, True)
        total = wb[lon].astype(f32)
        for d in range(1, N_LON):
            total = total + r1[d].astype(f32)
        c1[...] = total.astype(bf16)
        r2[lat] = c1[...]
        fan(hop2, N_LAT, False)

    def w_third():
        fan(hop2, N_LAT, True)
        total = r2[0].astype(f32)
        for d in range(1, N_LAT):
            total = total + r2[d].astype(f32)
        c2[...] = (total * scale[0]).astype(bf16)
        r3[lon] = c2[...]
        fan(hop3, N_LON, False)

    def rim2(e, row):
        main = ext2[e, 3:19].reshape(COLS, C)
        ra = one_hot(place == swap(lane))
        put_rim(ext2, e, dot(ra, main) + dot(rim_b[...], hc2[e]))

    def rims2(t, _):
        ra = one_hot(place == swap(lane))
        for j in (2 * t, 2 * t + 1):
            main = jnp.concatenate([ext2[2 * j + 3, 3:19].reshape(COLS, C), ext2[2 * j + 4, 3:19].reshape(COLS, C)], axis=-1)
            side = jnp.concatenate([hc2[2 * j + 3], hc2[2 * j + 4]], axis=-1)
            rim = dot(ra, main) + dot(rim_b[...], side)
            put_rim(ext2, 2 * j + 3, rim[:, :C])
            put_rim(ext2, 2 * j + 4, rim[:, C:])
        return 0

    cols2a.wait()
    lax.fori_loop(0, 4, rims2, 0)
    rims2(7, 0)

    def late_cols():
        cols2b.wait()
        lax.fori_loop(4, 7, rims2, 0)

    def edges2():
        rows2.wait()
        ra = one_hot(place == swap(lane))

        def rim(e):
            put_rim(ext2, e, dot(ra, ext2[e, 3:19].reshape(COLS, C)) + dot(rim_b[...], hc2[e]))

        def low():
            for e in range(3):
                rim(e)

        def inner():
            for e in range(3):
                rim(35 + e)

        def top():
            own = one_hot(swap(iota2((COLS, 1), 0)) == 255 - swap(lane))
            fa = one_hot(place == 255 - swap(lane))
            fb = one_hot(place == jnp.where(h32 < 16, -1 - h32, 287 - h32))
            for m in range(3):
                main = hr2[2 - m].reshape(COLS, C)
                fold[m, 3:19] = dot(own, main).astype(bf16).reshape(16, 16, C)
                put_rim(fold, m, dot(fa, main) + dot(fb, hc2[37 - m]))

        when(lk.low, low)
        when(lk.inner, inner)
        when(lk.top, top)

    def tap_sums(src, e, row, a, flip):
        for b in range(7):
            total = None
            for k0 in (0, 8):
                q = src[e, k0 + b] * ext[row + 3, 3 + k0]
                for k in range(k0 + 1, k0 + 8):
                    q = q + src[e, k + b] * ext[row + 3, 3 + k]
                total = q if total is None else total + q
            q = total.astype(f32)
            t = a * 7 + b
            gks[(48 - t) if flip else t] += q[:8] + q[8:]

    def finish(t, _):
        rest = jnp.concatenate([conv_first(ext2, taps, 2 * t, o) for o in (1, 0)], axis=-1)
        nat = dot(perm[...], (last_s[t].astype(f32) + rest).astype(bf16))
        for o in range(2):
            out[2 * t + o] = (cot[2 * t + o].astype(f32) + nat[:, (1 - o) * C:(2 - o) * C]).astype(bf16)
        return 0

    def back_step(n, _):
        when(n == 2, late_cols)
        when(n == 3, w_second)
        when(n == 5, w_third)
        when(n == NB - 2, edges2)
        row = back_block(n) * R
        conv = None
        for j in range(3):
            part = conv_part(ext2, row, wmat, True, 7 * j, 7 * j + 7)
            conv = part if conv is None else conv + part
            for t in range(28 * j // 3, 28 * (j + 1) // 3):
                tap_sums(ext2, row + t // 7 + t % 7, row + t // 7, t % 7, True)
        conv = conv.astype(bf16)
        for p in range(2):
            last_s[back_block(n) * 2 + p] = conv[p * COLS:(p + 1) * COLS]
        return 0

    lax.fori_loop(0, NB, back_step, 0)
    @pl.when(lk.top)
    def _():
        for t in range(3):
            for m in range(t + 1):
                tap_sums(fold, m, ROWS - 3 + t, 6 - t + m, False)

    rest = [jnp.sum(gks[t], axis=0, keepdims=True) for t in range(49)]
    rest += [jnp.sum(small[:8], axis=0, keepdims=True), jnp.sum(small[8:], axis=0, keepdims=True), jnp.zeros((13, C), f32)]
    c3[...] = jnp.concatenate(rest, axis=0).astype(bf16)
    fan(hop4, N_LON, False)
    q1[lon] = c3[...]

    def fold_conv():
        for t in range(3):
            acc = [None] * 16
            for m in range(t + 1):
                a = 6 - t + m
                for k in range(16):
                    p = fold[m, k] * taps[a * 7]
                    for b in range(1, 7):
                        p = p + fold[m, k + b] * taps[a * 7 + b]
                    p = p.astype(f32)
                    acc[k] = p if acc[k] is None else acc[k] + p
            row = ROWS - 3 + t
            side = slice((1 - row % 2) * C, (2 - row % 2) * C)
            last_s[row // 2, :, side] = (last_s[row // 2, :, side].astype(f32) + jnp.concatenate(acc, axis=0)).astype(bf16)

    when(lk.top, fold_conv)
    lax.fori_loop(0, ROWS // 4, finish, 0)
    fan(hop4, N_LON, True)
    total = q1[0].astype(f32)
    for d in range(1, N_LON):
        total = total + q1[d].astype(f32)
    c3[...] = total.astype(bf16)
    fan(hop5, N_LAT, False)
    q2[lat] = c3[...]
    lax.fori_loop(ROWS // 4, ROWS // 2, finish, 0)
    out_out = pltpu.make_async_copy(out, out_hbm, io.at[0])
    out_out.start()
    fan(hop3, N_LON, True)
    for j in range(4):
        for k in range(4):
            o_in[32 * k:32 * k + 32, j * C:(j + 1) * C] = r3[4 * k + j, 0:32].astype(f32)
        whole = jnp.concatenate([r3[4 * k + j, 32:SEG] for k in range(4)], axis=0).astype(f32)
        o_out[j * C:(j + 1) * C] = whole.T
    fan(hop5, N_LAT, True)
    total = q2[0].astype(f32)
    for d in range(1, N_LAT):
        total = total + q2[d].astype(f32)
    total = total * scale[0]
    for a in range(7):
        o_k[a] = total[7 * a:7 * a + 7]
    o_gain[...] = total[49:50]
    o_bias[...] = total[50:51]
    upd_out.wait()
    out_out.wait()


def hand_over(upd, grad, *refs):
    small, outs = refs[:5], refs[5:12]
    hold, sin, sout = refs[12:]
    chunks = [(k, i) for i in range(8) for k in range(2)]

    def move(k, i, inwards):
        rows = pl.ds(4 * i, 4)
        if inwards:
            return pltpu.make_async_copy((upd, grad)[k].at[rows], hold.at[k, rows], sin.at[k, i])
        return pltpu.make_async_copy(hold.at[k, rows], outs[k].at[rows], sout.at[k, i])

    for k, i in chunks:
        move(k, i, True).start()
    for a, b in zip(small, outs[2:]):
        b[...] = a[...]
    for k, i in chunks:
        move(k, i, True).wait()
        move(k, i, False).start()
    for k, i in chunks:
        move(k, i, False).wait()


def body(ocean_state, sea_mask, depth_kernel, conv_bias, norm_gain, w_in, w_out, cotangent):
    cells = COLS * ROWS * lax.axis_size("lat") * lax.axis_size("lon")
    scale = 1.0 / jnp.sqrt(jnp.full((1,), cells, f32))
    vm = pl.BlockSpec(memory_space=pltpu.VMEM)
    hbm = pl.BlockSpec(memory_space=pl.ANY)
    dma = pltpu.SemaphoreType.DMA
    V = pltpu.VMEM
    tile = jax.ShapeDtypeStruct((ROWS, COLS, C), bf16)
    upd, grad_state, o_in, o_out, o_k, o_bias, o_gain = pl.pallas_call(
        kernel,
        in_specs=[vm, vm, hbm, vm, vm, vm, vm, vm, pl.BlockSpec(memory_space=pltpu.SMEM)],
        out_specs=[hbm, hbm] + [vm] * 5,
        out_shape=[tile, tile, jax.ShapeDtypeStruct((C, HID), f32), jax.ShapeDtypeStruct((HID, C), f32),
                   jax.ShapeDtypeStruct((7, 7, C), f32), jax.ShapeDtypeStruct((1, C), f32), jax.ShapeDtypeStruct((1, C), f32)],
        scratch_shapes=[
            V((ROWS, COLS, C), bf16), V((ROWS, COLS, C), bf16), V((ROWS, COLS, C), bf16),
            V((38, 22, 16, C), bf16), V((38, 22, 16, C), bf16), V((28 * 256, 256), bf16), V((49, 16, C), bf16),
            V((COLS, COLS), bf16), V((96, COLS), bf16), V((96, 32), bf16), V((HID, C), bf16), V((C, HID), bf16),
            V((2 * COLS, 2 * C), f32), V((R, COLS, C), f32), V((ROWS, COLS, C), bf16), V((ROWS, COLS, C), bf16), V((ROWS // 2, COLS, 2 * C), bf16),
            V((ROWS, 32, C), bf16), V((6, COLS, C), bf16), V((ROWS + 6, 32, C), bf16),
            V((3, 16, 16, C), bf16), V((ROWS + 6, 32, C), bf16), V((3, 22, 16, C), bf16),
            V((C, HID), f32), V((C, HID), f32), V((49, 8, C), f32), V((16, C), f32),
            V((N_LON, SEG, C), bf16), V((SEG, C), bf16), V((SEG, C), bf16), V((SEG, C), bf16),
            V((N_LON, SEG, C), bf16), V((N_LAT, SEG, C), bf16), V((N_LON, SEG, C), bf16),
            V((N_LON, SEG, C), bf16), V((N_LAT, SEG, C), bf16),
            dma((2,)), dma((2,)), dma((2,)), dma((6,)), dma((6,)), dma((6,)), dma((6,)), dma((6,)), dma((6,)),
            dma((N_LON,)), dma((N_LON,)), dma((N_LAT,)), dma((N_LAT,)), dma((N_LON,)), dma((N_LON,)),
            dma((N_LON,)), dma((N_LON,)), dma((N_LAT,)), dma((N_LAT,))],
        compiler_params=pltpu.CompilerParams(collective_id=0, has_side_effects=True, vmem_limit_bytes=VLIM),
        name="block_step",
    )(ocean_state, sea_mask, cotangent, depth_kernel, conv_bias.reshape(1, C), norm_gain.reshape(1, C), w_in, w_out, scale)
    smalls = (o_k, o_bias, o_gain, o_in, o_out)
    upd, grad_state, o_k, o_bias, o_gain, o_in, o_out = pl.pallas_call(
        hand_over,
        in_specs=[hbm, hbm] + [vm] * 5,
        out_specs=[hbm, hbm] + [vm] * 5,
        out_shape=[tile, tile] + [jax.ShapeDtypeStruct(a.shape, a.dtype) for a in smalls],
        scratch_shapes=[V((2, ROWS, COLS, C), bf16), dma((2, 8)), dma((2, 8))],
        compiler_params=pltpu.CompilerParams(vmem_limit_bytes=VLIM),
        name="hand_over",
    )(upd, grad_state, *smalls)
    return upd, grad_state, o_k, o_bias.reshape(C), o_gain.reshape(C), o_in, o_out


def solution(mesh):
    tile = P("lat", "lon", None)
    return jax.shard_map(
        body,
        mesh=mesh,
        in_specs=(tile, P("lat", "lon"), P(), P(), P(), P(), P(), tile),
        out_specs=(tile, tile, P(), P(), P(), P(), P()),
        check_vma=False,
    )
```
